128 devices in a mesh: cell: 16 (over z, x), level: 4 (over y), rep: 2 (over core).
Axes of the slice: x: 4, y: 4, z: 4, core: 2. Of those that a mesh axis runs over, the one named last changes fastest.
Arguments:
- resident_pos: float32 [2, 32, 128, 2048], P(None, 'rep', 'level', 'cell'), may hold values from -0.5 to 0.5
- resident_strength: float32 [32, 128, 2048], P('rep', 'level', 'cell'), may hold values from -0.51 to 0.51
- mover_pos: float32 [2, 2, 4, 65536], P(None, 'rep', 'level', 'cell'), may hold values from -0.5 to 0.5
- mover_strength: float32 [2, 4, 65536], P('rep', 'level', 'cell'), may hold values from -0.51 to 0.51
- mover_owner: int32 [2, 4, 65536], P('rep', 'level', 'cell'), may hold values from 0 to 15, as said below
- mover_leaf: int32 [2, 4, 65536], P('rep', 'level', 'cell'), may hold values from 0 to 4095, as said below
- mover_slot: int32 [2, 4, 65536], P('rep', 'level', 'cell'), may hold values from 0 to 15
Outputs:
- velocity: float32 [2, 32, 128, 2048], P(None, 'rep', 'level', 'cell')
The draws below stay inside these ranges and needn't reach their ends.
Inputs may be any that keep to these rules, and one draw needn't show every extreme that they name: `mover_owner`: for one rep and level index, the 4096 movers of one device name one owner at most 1024 times, and one owner is named exactly 1024 times by every device. `mover_leaf`: leaf key y * 128 + x inside the owner's domain; for one rep and level index no (owner, leaf, slot) triple appears twice.
All inputs are finite; a program needn't handle non-finite values.
Results may differ from the reference program's by a relative error of at most 0.0003.
Values sent between devices are 32-bit elements; how exact they have to be, the bound alone decides.
No kernel may reach another device: no remote copies, remote signals or barrier semaphores. Data moves between devices by JAX's collectives and lax.ppermute only.
A program may use at most 192 MiB of HBM per device.

```python
import math
import jax
import jax.numpy as jnp
import numpy as np
from jax import lax

ORDER = 10
SLOT = 32
MOVE = 4096
SY = 32
SX = 128
HALF = 16
CAP = 1024
N_CELL = 16
N_LEVEL = 4
N_REP = 2


centre_weight = -5.0 / 3.0


def mover_routes(key):
    cell_count = N_CELL
    owned_slots = HALF * SX * SY
    leaves = SX * SY
    row_keys = jax.random.split(key, N_REP * N_LEVEL)

    def one_row(row_key):
        busy_key, pick_key, place_key = jax.random.split(row_key, 3)
        busiest = jax.random.randint(busy_key, (), 0, cell_count).astype(jnp.int32)
        others = (busiest + 1 + jnp.arange(cell_count - 1, dtype=jnp.int32)) % cell_count
        candidate = jnp.repeat(others, CAP)

        def one_source(source_key):
            pick_first, pick_second = jax.random.split(source_key)
            chosen = jax.random.permutation(pick_first, candidate)[:3 * CAP]
            named = jnp.concatenate([jnp.full((CAP,), busiest, jnp.int32), chosen.astype(jnp.int32)])
            return jax.random.permutation(pick_second, named)
        owners = jax.vmap(one_source)(jax.random.split(pick_key, cell_count))
        flat_owner = owners.reshape(-1)
        sort_order = jnp.argsort(flat_owner, stable=True)
        sorted_owner = flat_owner[sort_order]
        starts = jnp.searchsorted(sorted_owner, jnp.arange(cell_count, dtype=jnp.int32)).astype(jnp.int32)
        sorted_rank = jnp.arange(flat_owner.shape[0], dtype=jnp.int32) - starts[sorted_owner]
        rank_in_owner = jnp.zeros_like(flat_owner).at[sort_order].set(sorted_rank)

        def one_owner(owner_key):
            remaining = jax.random.permutation(owner_key, owned_slots - 2).astype(jnp.int32) + 1
            return jnp.concatenate([jnp.array([owned_slots - 1, 0], jnp.int32), remaining])
        places = jax.vmap(one_owner)(jax.random.split(place_key, cell_count))
        chosen_place = places[flat_owner, rank_in_owner]
        return (flat_owner, chosen_place % leaves, chosen_place // leaves)
    owners, leaf_keys, slot_keys = jax.vmap(one_row)(row_keys)
    out_shape = (N_REP, N_LEVEL, N_CELL * MOVE)
    return (owners.reshape(out_shape), leaf_keys.reshape(out_shape), slot_keys.reshape(out_shape))


def draw_mover_owner(key, part):
    return mover_routes(key)[0]


def draw_mover_leaf(key, part):
    return mover_routes(key)[1]


def draw_mover_slot(key, part):
    return mover_routes(key)[2]


def resident_corners(key):
    return jax.random.bernoulli(jax.random.fold_in(key, 101), 0.625, (SLOT, SY * N_LEVEL, SX * N_CELL))


def mover_corners(key):
    return jax.random.bernoulli(jax.random.fold_in(key, 102), 0.625, (N_REP, N_LEVEL, N_CELL * MOVE))


def corner_offsets(side_key, corners, jitter, centre):
    sides = jnp.where(jax.random.bernoulli(side_key, 0.5, jitter.shape), 1.0, -1.0)
    at_corner = sides * (0.5 - jitter)
    return jnp.where(corners[None], at_corner, centre).astype(jnp.float32)


def draw_resident_pos(key, part):
    corners = resident_corners(key)
    key = jax.random.fold_in(key, 23)
    side_key, jitter_key, centre_key = jax.random.split(key, 3)
    out_shape = (2,) + corners.shape
    jitter = jax.random.uniform(jitter_key, out_shape, jnp.float32, 0.0, 0.01)
    centre = jnp.clip(0.04 * jax.random.normal(centre_key, out_shape, jnp.float32), -0.1, 0.1)
    return corner_offsets(side_key, corners, jitter, centre)


def draw_mover_pos(key, part):
    corners = mover_corners(key)
    key = jax.random.fold_in(key, 24)
    side_key, jitter_key, centre_key = jax.random.split(key, 3)
    out_shape = (2,) + corners.shape
    jitter = jax.random.uniform(jitter_key, out_shape, jnp.float32, 0.0, 0.01)
    centre = jnp.clip(0.04 * jax.random.normal(centre_key, out_shape, jnp.float32), -0.1, 0.1)
    return corner_offsets(side_key, corners, jitter, centre)


def draw_resident_strength(key, part):
    corners = resident_corners(key)
    key = jax.random.fold_in(key, 21)
    sign_key, size_key = jax.random.split(key)
    out_shape = corners.shape
    leaf_sign = jnp.where(jax.random.bernoulli(sign_key, 0.5, out_shape[1:]), 1.0, -1.0)[None]
    weight = jnp.where(corners, 1.0, centre_weight)
    sizes = jnp.exp(jax.random.uniform(size_key, out_shape, jnp.float32, math.log(0.15), math.log(0.3)))
    return (leaf_sign * sizes * weight).astype(jnp.float32)


def draw_mover_strength(key, part):
    corners = mover_corners(key)
    key = jax.random.fold_in(key, 22)
    sign_key, size_key = jax.random.split(key)
    out_shape = corners.shape
    signs = jnp.where(jax.random.bernoulli(sign_key, 0.5, out_shape), 1.0, -1.0)
    weight = jnp.where(corners, 1.0, centre_weight)
    sizes = jnp.exp(jax.random.uniform(size_key, out_shape, jnp.float32, math.log(0.15), math.log(0.3)))
    return (signs * sizes * weight).astype(jnp.float32)


def setup_inputs(seed: int = 0) -> dict:
    splits = jax.random.split(jax.random.key(seed), 8)
    return {
        "resident_pos": draw_resident_pos(jax.random.fold_in(splits[7], 71), 0),
        "resident_strength": draw_resident_strength(jax.random.fold_in(splits[7], 71), 0),
        "mover_pos": draw_mover_pos(jax.random.fold_in(splits[7], 71), 0),
        "mover_strength": draw_mover_strength(jax.random.fold_in(splits[7], 71), 0),
        "mover_owner": draw_mover_owner(jax.random.fold_in(splits[7], 71), 0),
        "mover_leaf": draw_mover_leaf(jax.random.fold_in(splits[7], 71), 0),
        "mover_slot": draw_mover_slot(jax.random.fold_in(splits[7], 71), 0),
    }


precise = lax.Precision.HIGHEST
blob_square = 0.09


def real_form(matrix):
    top_rows = np.concatenate([matrix.real, -matrix.imag], axis=1)
    low_rows = np.concatenate([matrix.imag, matrix.real], axis=1)
    return np.concatenate([top_rows, low_rows], axis=0)


def child_offset(parity_x, parity_y):
    return complex((parity_x - 0.5) / 2.0, (parity_y - 0.5) / 2.0)


def upward_table(parity_x, parity_y):
    offset = child_offset(parity_x, parity_y)
    matrix = np.zeros((ORDER, ORDER), complex)
    for k in range(ORDER):
        for m in range(k + 1):
            matrix[k, m] = math.comb(k, m) * 0.5 ** m * offset ** (k - m)
    return real_form(matrix)


def downward_table(parity_x, parity_y):
    offset = child_offset(parity_x, parity_y)
    matrix = np.zeros((ORDER, ORDER), complex)
    for m in range(ORDER):
        for l in range(m, ORDER):
            matrix[m, l] = 0.5 ** (m + 1) * math.comb(l, m) * offset ** (l - m)
    return real_form(matrix)


def far_table(step_x, step_y):
    distance = complex(step_x, step_y)
    matrix = np.zeros((ORDER, ORDER), complex)
    for l in range(ORDER):
        for k in range(ORDER):
            matrix[l, k] = (-1) ** (k + 1) * math.comb(k + l, l) * distance ** (-(k + l + 1))
    return real_form(matrix)


def apply_matrix(matrix, level_field):
    return jnp.einsum("ij,jyx->iyx", jnp.asarray(matrix, dtype=jnp.float32), level_field, precision=precise)


def upward(level_field):
    summed = None
    for parity_y in (0, 1):
        for parity_x in (0, 1):
            product = apply_matrix(upward_table(parity_x, parity_y), level_field[:, parity_y::2, parity_x::2])
            summed = product if summed is None else summed + product
    return summed


def downward(parent):
    channels, cells_y, cells_x = parent.shape
    pieces = jnp.stack([jnp.stack([apply_matrix(downward_table(parity_x, parity_y), parent) for parity_x in (0, 1)]) for parity_y in (0, 1)])
    return pieces.transpose(2, 3, 0, 4, 1).reshape(channels, 2 * cells_y, 2 * cells_x)


def interactions(level_field, at_top):
    channels, cells_y, cells_x = level_field.shape
    reach_y = cells_y - 1 if at_top else 3
    reach_x = cells_x - 1 if at_top else 3
    padded = jnp.pad(level_field, ((0, 0), (reach_y, reach_y), (reach_x, reach_x)))
    parity_y = (jnp.arange(cells_y, dtype=jnp.int32) % 2)[:, None]
    parity_x = (jnp.arange(cells_x, dtype=jnp.int32) % 2)[None, :]
    summed = jnp.zeros(level_field.shape, jnp.float32)
    for step_y in range(-reach_y, reach_y + 1):
        for step_x in range(-reach_x, reach_x + 1):
            if max(abs(step_x), abs(step_y)) <= 1:
                continue
            source = padded[:, reach_y + step_y:reach_y + step_y + cells_y, reach_x + step_x:reach_x + step_x + cells_x]
            product = apply_matrix(far_table(step_x, step_y), source)
            if not at_top:
                inside = (parity_x + step_x >= -2) & (parity_x + step_x <= 3) & (parity_y + step_y >= -2) & (parity_y + step_y <= 3)
                product = product * inside.astype(jnp.float32)[None]
            summed = summed + product
    return summed


def moments(pos_x, pos_y, strength):
    real_power = jnp.ones_like(pos_x)
    imag_power = jnp.zeros_like(pos_x)
    real_rows = []
    imag_rows = []
    for k in range(ORDER):
        real_rows.append(jnp.sum(strength * real_power, axis=0))
        imag_rows.append(jnp.sum(strength * imag_power, axis=0))
        real_power, imag_power = real_power * pos_x - imag_power * pos_y, real_power * pos_y + imag_power * pos_x
    return jnp.stack(real_rows + imag_rows)


def evaluate(local_field, pos_x, pos_y):
    real_acc = jnp.broadcast_to(local_field[ORDER - 1], pos_x.shape)
    imag_acc = jnp.broadcast_to(local_field[2 * ORDER - 1], pos_x.shape)
    for l in range(ORDER - 2, -1, -1):
        real_acc, imag_acc = (real_acc * pos_x - imag_acc * pos_y + local_field[l],
                              real_acc * pos_y + imag_acc * pos_x + local_field[ORDER + l])
    return real_acc, imag_acc


def near_field(particles):
    slot_count, cells_y, cells_x = particles.shape[1:]
    padded = jnp.pad(particles, ((0, 0), (0, 0), (1, 1), (1, 1)))
    band_rows = 8
    keep_mask = (1.0 - jnp.eye(slot_count, dtype=jnp.float32))[:, :, None, None]

    def one_band(row_start):
        target = lax.dynamic_slice_in_dim(particles, row_start, band_rows, 2)
        real_sum = jnp.zeros((slot_count, band_rows, cells_x), jnp.float32)
        imag_sum = jnp.zeros((slot_count, band_rows, cells_x), jnp.float32)
        for step_y in (-1, 0, 1):
            row_band = lax.dynamic_slice_in_dim(padded, row_start + 1 + step_y, band_rows, 2)
            for step_x in (-1, 0, 1):
                source = row_band[:, :, :, 1 + step_x:1 + step_x + cells_x]
                gap_x = target[0][:, None] - source[0][None] - step_x
                gap_y = target[1][:, None] - source[1][None] - step_y
                weight = source[2][None] / (gap_x * gap_x + gap_y * gap_y + blob_square)
                if step_x == 0 and step_y == 0:
                    weight = weight * keep_mask
                real_sum = real_sum + jnp.sum(weight * gap_x, axis=1)
                imag_sum = imag_sum - jnp.sum(weight * gap_y, axis=1)
        return jnp.stack([real_sum, imag_sum])

    starts = jnp.arange(0, cells_y, band_rows, dtype=jnp.int32)
    bands = lax.map(one_band, starts)
    return bands.transpose(1, 2, 0, 3, 4).reshape(2, slot_count, cells_y, cells_x)


def reference(resident_pos, resident_strength, mover_pos, mover_strength, mover_owner, mover_leaf, mover_slot):
    wide_x = SX * N_CELL
    wide_y = SY * N_LEVEL
    rep_index = jnp.arange(N_REP, dtype=jnp.int32)[:, None, None]
    level_index = jnp.arange(N_LEVEL, dtype=jnp.int32)[None, :, None]
    slot_index = rep_index * HALF + mover_slot
    row_index = level_index * SY + mover_leaf // SX
    column_index = mover_owner * SX + mover_leaf % SX
    flat_index = ((slot_index * wide_y + row_index) * wide_x + column_index).reshape(-1)
    resident = jnp.concatenate([resident_pos.reshape(2, -1), resident_strength.reshape(1, -1)])
    incoming = jnp.concatenate([mover_pos.reshape(2, -1), mover_strength.reshape(1, -1)])
    particles = resident.at[:, flat_index].set(incoming).reshape(3, SLOT, wide_y, wide_x)
    level_fields = [moments(particles[0], particles[1], particles[2])]
    top_level = min(wide_x, wide_y).bit_length() - 1
    for k in range(top_level):
        level_fields.append(upward(level_fields[-1]))
    local_field = interactions(level_fields[top_level], True)
    for k in range(top_level - 1, -1, -1):
        local_field = interactions(level_fields[k], False) + downward(local_field)
    far_real, far_imag = evaluate(local_field, particles[0], particles[1])
    near = near_field(particles)
    real_part = near[0] + far_real
    imag_part = near[1] + far_imag
    return jnp.stack([imag_part, real_part]) / (2.0 * math.pi)
```

```python
import functools
import math

import jax
import jax.numpy as jnp
import numpy as np
from jax import lax
from jax.experimental import pallas as pl
from jax.experimental.pallas import tpu as pltpu
from jax.sharding import PartitionSpec as P

ORDER = 10
CHAN = 2 * ORDER
FAMILY = 4 * CHAN
CAP = 1024
BLOB = 0.09
LANES = 128
HEIGHTS = (16, 8, 4, 2, 1)
WIDTHS = (64, 32, 16, 8, 4)
OFFSETS = (0, 16, 24, 28, 30)
ROWS = 31
PACKS = (None, 0, 34, 52, 62)
VMEM = 56 * 2**20

f32 = jnp.float32
bf16 = jnp.bfloat16
precise = lax.Precision.HIGHEST


def real_form(matrix):
    top_rows = np.concatenate([matrix.real, -matrix.imag], axis=1)
    low_rows = np.concatenate([matrix.imag, matrix.real], axis=1)
    return np.concatenate([top_rows, low_rows], axis=0)


def child_offset(parity_x, parity_y):
    return complex((parity_x - 0.5) / 2.0, (parity_y - 0.5) / 2.0)


def upward_table(parity_x, parity_y):
    offset = child_offset(parity_x, parity_y)
    matrix = np.zeros((ORDER, ORDER), complex)
    for k in range(ORDER):
        for m in range(k + 1):
            matrix[k, m] = math.comb(k, m) * 0.5**m * offset ** (k - m)
    return real_form(matrix)


def downward_table(parity_x, parity_y):
    offset = child_offset(parity_x, parity_y)
    matrix = np.zeros((ORDER, ORDER), complex)
    for m in range(ORDER):
        for l in range(m, ORDER):
            matrix[m, l] = 0.5 ** (m + 1) * math.comb(l, m) * offset ** (l - m)
    return real_form(matrix)


def far_table(step_x, step_y):
    distance = complex(step_x, step_y)
    matrix = np.zeros((ORDER, ORDER), complex)
    for l in range(ORDER):
        for k in range(ORDER):
            matrix[l, k] = (-1) ** (k + 1) * math.comb(k + l, l) * distance ** (-(k + l + 1))
    return real_form(matrix)


def family(parity_x, parity_y):
    first = (2 * parity_x + parity_y) * CHAN
    return slice(first, first + CHAN)


def upward_family():
    table = np.zeros((CHAN, FAMILY))
    for b in (0, 1):
        for a in (0, 1):
            table[:, family(b, a)] = upward_table(b, a)
    return table


def downward_family():
    table = np.zeros((FAMILY, CHAN))
    for b in (0, 1):
        for a in (0, 1):
            table[family(b, a), :] = downward_table(b, a)
    return table


def far_family():
    table = np.zeros((3, FAMILY, 3, FAMILY))
    for dx in (-1, 0, 1):
        for dy in (-1, 0, 1):
            for bt in (0, 1):
                for at in (0, 1):
                    for bs in (0, 1):
                        for as_ in (0, 1):
                            step_x = 2 * dx + bs - bt
                            step_y = 2 * dy + as_ - at
                            if max(abs(step_x), abs(step_y)) >= 2:
                                table[dx + 1, family(bt, at), dy + 1, family(bs, as_)] = far_table(
                                    step_x, step_y
                                )
    return table.reshape(3 * FAMILY, 3 * FAMILY)


def coarse_tables():
    far5 = {}
    to_top = np.zeros((4, LANES, LANES))
    near5 = np.zeros((4, 12, LANES, LANES))
    from_top = np.zeros((4, LANES, LANES))
    lane = lambda column: np.arange(CHAN) * 4 + column
    for row in range(4):
        for column in range(4):
            lift = upward_table(column // 2, row // 2) @ upward_table(column % 2, row % 2)
            to_top[row][np.ix_(lane(column), np.arange(CHAN))] = lift.T
            drop = downward_table(column % 2, row % 2) @ downward_table(column // 2, row // 2)
            from_top[row][np.ix_(np.arange(CHAN), lane(column))] = drop.T
    for row in range(4):
        for column in range(4):
            down = downward_table(column % 2, row % 2)
            x = 4 + column
            for step in range(3):
                for other_row in range(4):
                    for other in range(4):
                        u = 4 * step + other
                        total = np.zeros((CHAN, CHAN))
                        if abs(u // 2 - x // 2) <= 1:
                            if max(abs(u - x), abs(other_row - row)) >= 2:
                                total += far_table(u - x, other_row - row)
                        if abs(u // 2 - x // 2) >= 2:
                            key = (u // 2 - x // 2, other_row // 2 - row // 2)
                            if key not in far5:
                                far5[key] = far_table(*key)
                            total += down @ far5[key] @ upward_table(other % 2, other_row % 2)
                        near5[row, step * 4 + other_row][np.ix_(lane(other), lane(column))] += total.T
    top = np.zeros((LANES, 32 * 32))
    for step in range(-15, 16):
        if abs(step) >= 2:
            top[:CHAN, (step + 15) * 32 : (step + 15) * 32 + CHAN] = far_table(step, 0).T
    return to_top, near5, from_top, top


def halves_np(table):
    high = np.asarray(table, np.float32).astype(jnp.bfloat16)
    low = (np.asarray(table, np.float32) - high.astype(np.float32)).astype(jnp.bfloat16)
    return high, low


def split_lanes():
    table = np.zeros((LANES, LANES), np.float32)
    x = np.arange(LANES)
    table[x, 64 * (x % 2) + x // 2] = 1.0
    return np.concatenate([table, table], axis=0).astype(jnp.bfloat16)


def join_lanes():
    table = np.zeros((2, LANES, LANES), np.float32)
    x = np.arange(64)
    table[0, x, 2 * x] = 1.0
    table[1, x, 2 * x + 1] = 1.0
    table = table.reshape(2 * LANES, LANES)
    return np.concatenate([table, table], axis=0).astype(jnp.bfloat16)


def quarter_lanes():
    k = np.arange(LANES)
    return (k[:, None] % 4 == k[None, :]).astype(np.float32)


def halves(value):
    high = value.astype(bf16)
    return high, (value - high.astype(f32)).astype(bf16)


def dot(left, right):
    return jnp.dot(left, right, preferred_element_type=f32)


def lane_index(rows):
    return lax.broadcasted_iota(jnp.int32, (rows, LANES), 1)


def whole(shape):
    return pl.BlockSpec(shape, lambda *_: (0,) * len(shape))


def upward_kernel(
    own, other, split_ref, lift_ref, spread_ref, cells, packed, coarse, mom, raw
):
    for tile in range(4):
        rows = pl.ds(8 * tile, 8)

        def add_slot(j, sums):
            for ref in (own, other):
                x, y, re = ref[0, j, rows, :], ref[1, j, rows, :], ref[2, j, rows, :]
                real, imag = list(sums[:ORDER]), list(sums[ORDER:])
                real[0] = real[0] + re
                im = re * y
                re = re * x
                real[1] = real[1] + re
                imag[1] = imag[1] + im
                for k in range(2, ORDER):
                    re, im = re * x - im * y, re * y + im * x
                    real[k] = real[k] + re
                    imag[k] = imag[k] + im
                sums = tuple(real + imag)
            return sums

        sums = lax.fori_loop(
            0, 16, add_slot, tuple(jnp.zeros((8, LANES), f32) for _ in range(CHAN)), unroll=2
        )
        for c in range(CHAN):
            mom[pl.ds(8 * tile * CHAN + c, 8, stride=CHAN), :] = sums[c]

    lane40 = lane_index(40)
    lane80 = lane_index(FAMILY)
    first = jnp.zeros((FAMILY, LANES), f32)
    last = jnp.zeros((FAMILY, LANES), f32)
    for k, height in enumerate(HEIGHTS):
        source = mom[...] if k == 0 else raw[pl.ds(0, 40 * height), :]
        spread = dot(jnp.concatenate(halves(source), axis=1), split_ref[...])
        parents = []
        for row in range(height):
            block = spread[40 * row : 40 * row + 40]
            even = jnp.where(lane40 < 64, block, 0.0)
            odd = jnp.where(lane40 < 64, pltpu.roll(block, 64, 1), 0.0)
            parent = jnp.concatenate([even, odd], axis=0)
            index = OFFSETS[k] + row
            cells[pl.ds(FAMILY * index, FAMILY), :] = parent
            first = jnp.where(lane80 == index, pltpu.roll(parent, index, 1), first)
            last = jnp.where(
                lane80 == index, pltpu.roll(parent, (index - WIDTHS[k] + 1) % LANES, 1), last
            )
            parents.append(parent)
        high, low = halves(jnp.concatenate(parents, axis=1))
        lifted = dot(lift_ref[...], jnp.concatenate([high, low, high], axis=0))
        for row in range(height):
            raw[pl.ds(CHAN * row, CHAN), :] = lifted[:CHAN, LANES * row : LANES * (row + 1)]
    packed[0, pl.ds(32, FAMILY), :] = first
    packed[1, pl.ds(32, FAMILY), :] = last

    four = jnp.dot(raw[pl.ds(0, 24), :], spread_ref[...], precision=precise)
    row24 = lax.broadcasted_iota(jnp.int32, (24, LANES), 0)
    line = jnp.sum(jnp.where((lane_index(24) // 4 == row24) & (row24 < CHAN), four, 0.0), axis=0, keepdims=True)
    coarse[...] = jnp.broadcast_to(line, coarse.shape)

    lane32 = lane_index(32)

    def edge(j, sides):
        left, right = sides
        for half, ref in enumerate((own, other)):
            for comp in range(3):
                m = comp * 32 + half * 16 + j
                value = ref[comp, j]
                left = jnp.where(lane32 == m, pltpu.roll(value, m, 1), left)
                right = jnp.where(lane32 == m, pltpu.roll(value, m + 1, 1), right)
        return left, right

    zero = jnp.zeros((32, LANES), f32)
    left, right = lax.fori_loop(0, 16, edge, (zero, zero))
    packed[0, pl.ds(0, 32), :] = left
    packed[1, pl.ds(0, 32), :] = right


def ring_columns(parent, k, index, from_left, from_right, lane):
    width = WIDTHS[k]
    parent = jnp.where(lane == LANES - 1, pltpu.roll(from_left, (LANES - 1 - index) % LANES, 1), parent)
    return jnp.where(lane == width, pltpu.roll(from_right, (width - index) % LANES, 1), parent)


def rows_kernel(own, other, cells, from_left, from_right, out):
    lane80 = lane_index(FAMILY)
    left, right = from_left[pl.ds(32, FAMILY), :], from_right[pl.ds(32, FAMILY), :]
    for side in (0, 1):
        row = 31 * side
        for comp in range(3):
            for half, ref in enumerate((own, other)):
                for j in range(16):
                    out[side, pl.ds(comp * 32 + half * 16 + j, 1), :] = ref[comp, j, pl.ds(row, 1), :]
        out[side, pl.ds(96, 1), :] = from_left[pl.ds(row, 1), :]
        out[side, pl.ds(97, 1), :] = from_right[pl.ds(row, 1), :]
        out[side, pl.ds(98, 6), :] = jnp.zeros((6, LANES), f32)
        packed = jnp.zeros((FAMILY, LANES), f32)
        for k, height in enumerate(HEIGHTS):
            index = OFFSETS[k] + (height - 1) * side
            parent = cells[pl.ds(FAMILY * index, FAMILY), :]
            parent = ring_columns(parent, k, index, left, right, lane80)
            if k == 0:
                out[side, pl.ds(104, FAMILY), :] = parent
            else:
                moved = pltpu.roll(parent, PACKS[k] + 1, 1)
                inside = (lane80 >= PACKS[k]) & (lane80 < PACKS[k] + WIDTHS[k] + 2)
                packed = jnp.where(inside, moved, packed)
        out[side, pl.ds(104 + FAMILY, FAMILY), :] = packed


GROUP = 8


def near_kernel(own, other, from_left, from_right, above, below, out, src):
    lane32 = lane_index(32)
    lane1 = lane_index(1)

    for comp in range(3):
        for half, ref in enumerate((own, other)):

            def frame(j, _, comp=comp, half=half, ref=ref):
                m = comp * 32 + half * 16 + j
                back = (LANES - m) % LANES if isinstance(m, int) else LANES - m
                value = ref[comp, j]
                rows = (value, above[pl.ds(m, 1), :], below[pl.ds(m, 1), :])
                lefts = (from_left[pl.ds(0, 32), :], above[pl.ds(96, 1), :], below[pl.ds(96, 1), :])
                rights = (from_right[pl.ds(0, 32), :], above[pl.ds(97, 1), :], below[pl.ds(97, 1), :])
                for part in range(3):
                    place = (pl.ds(8, 32), pl.ds(7, 1), pl.ds(40, 1))[part]
                    lane = lane32 if part == 0 else lane1
                    middle = rows[part]
                    before = jnp.where(
                        lane == 0, pltpu.roll(lefts[part], back, 1), pltpu.roll(middle, 1, 1)
                    )
                    after = jnp.where(
                        lane == LANES - 1,
                        pltpu.roll(rights[part], LANES - 1 - m, 1),
                        pltpu.roll(middle, LANES - 1, 1),
                    )
                    if comp == 0:
                        before = before - 1.0
                        after = after + 1.0
                    src[0, m, place, :] = before
                    src[1, m, place, :] = middle
                    src[2, m, place, :] = after
                return 0

            lax.fori_loop(0, 16, frame, 0)

    for tile in range(4):
        for group in range(16 // GROUP):
            tx = [own[0, group * GROUP + i, pl.ds(8 * tile, 8), :] for i in range(GROUP)]
            ty0 = [own[1, group * GROUP + i, pl.ds(8 * tile, 8), :] for i in range(GROUP)]
            acc = tuple(jnp.zeros((8, LANES), f32) for _ in range(2 * GROUP))
            for dy in (-1, 0, 1):
                ty = [value - float(dy) for value in ty0] if dy else ty0
                rows = pl.ds(8 + 8 * tile + dy, 8)
                for dx in range(3):

                    def pairs(j, acc, dx=dx, rows=rows, ty=ty, tx=tx):
                        acc = list(acc)
                        sx, sy, q = src[dx, j, rows, :], src[dx, 32 + j, rows, :], src[dx, 64 + j, rows, :]
                        for i in range(GROUP):
                            gap_x = tx[i] - sx
                            gap_y = ty[i] - sy
                            weight = q * (1.0 / (gap_x * gap_x + (gap_y * gap_y + BLOB)))
                            acc[i] = acc[i] + weight * gap_x
                            acc[GROUP + i] = acc[GROUP + i] + weight * gap_y
                        return tuple(acc)

                    acc = lax.fori_loop(0, 32, pairs, acc, unroll=4)
            for i in range(GROUP):
                out[0, group * GROUP + i, pl.ds(8 * tile, 8), :] = acc[i]
                out[1, group * GROUP + i, pl.ds(8 * tile, 8), :] = acc[GROUP + i]


def far_kernel(
    place, own, near, cells, from_left, from_right, above, below, gathered,
    far_ref, drop_ref, join_ref, spread_ref, to_top, near5, from_top, top_ref,
    out, high, low, fars, paired, joined_ref, loc,
):
    cell = place[0]
    level = place[1]
    tops = jnp.zeros((16, LANES), f32)
    for row in range(4):
        tops = tops + jnp.dot(gathered[pl.ds(row, 16, stride=4), :], to_top[row], precision=precise)
    spread = jnp.dot(tops, top_ref[...], precision=precise)
    source = lax.broadcasted_iota(jnp.int32, (16, 1024), 0)
    step = lax.broadcasted_iota(jnp.int32, (16, 1024), 1) // 32
    line = jnp.sum(jnp.where(step == source - cell + 15, spread, 0.0), axis=0, keepdims=True)
    total = line[:, :LANES]
    for block in range(1, 8):
        total = total + line[:, LANES * block : LANES * (block + 1)]
    total = jnp.broadcast_to(total, (8, LANES))
    total = total + pltpu.roll(total, 64, 1)
    total = total + pltpu.roll(total, 32, 1)
    total = jnp.where(lane_index(8) < CHAN, total, 0.0)
    five = jnp.dot(total, from_top[0], precision=precise)
    for step in range(3):
        there = cell + step - 1
        valid = jnp.where((there >= 0) & (there < 16), 1.0, 0.0)
        there = jnp.clip(there, 0, 15)
        for row in range(4):
            value = jnp.broadcast_to(gathered[pl.ds(there * 4 + row, 1), :], (8, LANES)) * valid
            five = five + jnp.dot(value, near5[0, step * 4 + row], precision=precise)
    five = jnp.broadcast_to(five[0:1], (32, LANES))
    row32 = lax.broadcasted_iota(jnp.int32, (32, LANES), 0)
    five = jnp.where((lane_index(32) // 4 == row32) & (row32 < CHAN), five, 0.0)
    loc[...] = jnp.zeros(loc.shape, f32)
    loc[pl.ds(0, 32), pl.ds(0, LANES)] = jnp.dot(five, spread_ref[...], precision=precise)

    lane80 = lane_index(FAMILY)
    left, right = from_left[pl.ds(32, FAMILY), :], from_right[pl.ds(32, FAMILY), :]
    start = 0
    starts = []
    for k, height in enumerate(HEIGHTS):
        starts.append(start)
        for row in range(-1, height + 1):
            if row in (-1, height):
                ref = above if row == -1 else below
                if k == 0:
                    parent = ref[pl.ds(104, FAMILY), :]
                else:
                    packed = ref[pl.ds(104 + FAMILY, FAMILY), :]
                    parent = pltpu.roll(packed, LANES - PACKS[k] - 1, 1)
                    parent = jnp.where((lane80 <= WIDTHS[k]) | (lane80 == LANES - 1), parent, 0.0)
            else:
                index = OFFSETS[k] + row
                parent = cells[pl.ds(FAMILY * index, FAMILY), :]
                parent = ring_columns(parent, k, index, left, right, lane80)
            part_high, part_low = halves(parent)
            high[pl.ds(FAMILY * start, FAMILY), :] = part_high
            low[pl.ds(FAMILY * start, FAMILY), :] = part_low
            start += 1

    def far_rows(k, rows):
        both = []
        for ref in (high, low):
            both.append(
                jnp.concatenate(
                    [ref[pl.ds(FAMILY * (starts[k] + row), 3 * FAMILY), :] for row in rows], axis=1
                )
            )
        size = 3 * FAMILY
        product = dot(far_ref[...], both[0])
        product = product[:size] + product[size:] + dot(far_ref[pl.ds(0, size), :], both[1])
        for place_, row in enumerate(rows):
            part = product[:, LANES * place_ : LANES * (place_ + 1)]
            fars[pl.ds(FAMILY * (OFFSETS[k] + row), FAMILY), :] = (
                part[FAMILY : 2 * FAMILY]
                + pltpu.roll(part[:FAMILY], 1, 1)
                + pltpu.roll(part[2 * FAMILY :], LANES - 1, 1)
            )

    for k, height in enumerate(HEIGHTS):
        for row in range(0, height, 2):
            far_rows(k, (row, row + 1) if height > 1 else (row,))

    for k in range(4, -1, -1):
        height = HEIGHTS[k]
        part_high, part_low = halves(loc[:, pl.ds(0, LANES * height)])
        dropped = dot(drop_ref[...], jnp.concatenate([part_high, part_low, part_high], axis=0))
        for row in range(height):
            here = dropped[:, LANES * row : LANES * (row + 1)] + fars[pl.ds(FAMILY * (OFFSETS[k] + row), FAMILY), :]
            paired[pl.ds(40 * row, 40), :] = jnp.concatenate([here[:40], here[40:]], axis=1)
        part_high, part_low = halves(paired[pl.ds(0, 40 * height), :])
        joined = dot(jnp.concatenate([part_high, part_low], axis=1), join_ref[...])
        joined_ref[pl.ds(0, 40 * height), :] = joined
        if k > 0:
            for row in range(2 * height):
                loc[pl.ds(0, CHAN), pl.ds(LANES * row, LANES)] = joined_ref[pl.ds(CHAN * row, CHAN), :]

    scale = 1.0 / (2.0 * math.pi)
    for tile in range(4):
        rows = pl.ds(8 * tile, 8)
        terms = [joined_ref[pl.ds(8 * tile * CHAN + c, 8, stride=CHAN), :] for c in range(CHAN)]

        def value(j, _, terms=terms, rows=rows):
            x, y = own[0, j, rows, :], own[1, j, rows, :]
            re, im = terms[ORDER - 1], terms[CHAN - 1]
            for l in range(ORDER - 2, -1, -1):
                re, im = re * x - im * y + terms[l], re * y + im * x + terms[ORDER + l]
            out[0, j, rows, :] = (im - near[1, j, rows, :]) * scale
            out[1, j, rows, :] = (re + near[0, j, rows, :]) * scale
            return 0

        lax.fori_loop(0, 16, value, 0, unroll=2)


def params():
    return pltpu.CompilerParams(vmem_limit_bytes=VMEM)


def shape(*sizes):
    return jax.ShapeDtypeStruct(sizes, f32)


def neighbours(value, axis, step):
    size = lax.axis_size(axis)
    return lax.ppermute(value, axis, [(i, i + step) for i in range(size) if 0 <= i + step < size])


def fields(own):
    other = lax.ppermute(own, "rep", [(0, 1), (1, 0)])
    lift_high, lift_low = halves_np(upward_family())
    lift = np.zeros((32, 3 * FAMILY), jnp.bfloat16)
    lift[:CHAN] = np.concatenate([lift_high, lift_high, lift_low], axis=1)
    cells, packed, coarse = pl.pallas_call(
        upward_kernel,
        out_shape=(shape(ROWS * FAMILY, LANES), shape(2, 32 + FAMILY, LANES), shape(64, LANES)),
        scratch_shapes=[pltpu.VMEM((640, LANES), f32), pltpu.VMEM((320, LANES), f32)],
        compiler_params=params(),
        name="upward",
    )(own, other, jnp.asarray(split_lanes()), jnp.asarray(lift), jnp.asarray(quarter_lanes().T.copy()))
    from_left = neighbours(packed[1], "cell", 1)
    from_right = neighbours(packed[0], "cell", -1)
    gathered = lax.all_to_all(coarse, ("cell", "level"), 0, 0, tiled=True)
    rows = pl.pallas_call(
        rows_kernel,
        out_shape=shape(2, 104 + 2 * FAMILY, LANES),
        compiler_params=params(),
        name="rows",
    )(own, other, cells, from_left, from_right)
    above = neighbours(rows[1], "level", 1)
    below = neighbours(rows[0], "level", -1)
    near = pl.pallas_call(
        near_kernel,
        out_shape=shape(2, 16, 32, LANES),
        scratch_shapes=[pltpu.VMEM((3, 96, 48, LANES), f32)],
        compiler_params=params(),
        name="near",
    )(own, other, from_left, from_right, above, below)
    far_high, far_low = halves_np(far_family())
    drop_table = np.zeros((FAMILY, 32))
    drop_table[:, :CHAN] = downward_family()
    drop_high, drop_low = halves_np(drop_table)
    to_top, near5, from_top, top = coarse_tables()
    tables = [
        np.concatenate([far_high, far_low], axis=0),
        np.concatenate([drop_high, drop_high, drop_low], axis=1),
        join_lanes(),
        quarter_lanes(),
        to_top.astype(np.float32),
        near5.astype(np.float32),
        from_top.astype(np.float32),
        top.astype(np.float32),
    ]
    operands = [own, near, cells, from_left, from_right, above, below, gathered] + [
        jnp.asarray(table) for table in tables
    ]
    specs = [whole(value.shape) for value in operands]
    specs[13] = pl.BlockSpec((1, 12, LANES, LANES), lambda i, place: (place[1], 0, 0, 0))
    specs[14] = pl.BlockSpec((1, LANES, LANES), lambda i, place: (place[1], 0, 0))
    place = jnp.stack([lax.axis_index("cell"), lax.axis_index("level")]).astype(jnp.int32)
    return pl.pallas_call(
        far_kernel,
        grid_spec=pltpu.PrefetchScalarGridSpec(
            num_scalar_prefetch=1,
            grid=(1,),
            in_specs=specs,
            out_specs=whole((2, 16, 32, LANES)),
            scratch_shapes=[
                pltpu.VMEM((41 * FAMILY, LANES), bf16),
                pltpu.VMEM((41 * FAMILY, LANES), bf16),
                pltpu.VMEM((ROWS * FAMILY, LANES), f32),
                pltpu.VMEM((640, 2 * LANES), f32),
                pltpu.VMEM((640, LANES), f32),
                pltpu.VMEM((32, 16 * LANES), f32),
            ],
        ),
        out_shape=shape(2, 16, 32, LANES),
        compiler_params=params(),
        name="far",
    )(place, *operands)


def local(
    resident_pos, resident_strength, mover_pos, mover_strength, mover_owner, mover_leaf, mover_slot
):
    cell_count = lax.axis_size("cell")
    half_slots, cells_y, cells_x = resident_strength.shape
    leaves = cells_y * cells_x
    owner_cell = mover_owner.reshape(-1)
    address = mover_slot.reshape(-1) * leaves + mover_leaf.reshape(-1)
    peer_ids = jnp.arange(cell_count, dtype=jnp.int32)
    onehot = (owner_cell[:, None] == peer_ids[None, :]).astype(jnp.int32)
    rank_in_owner = jnp.sum(jnp.cumsum(onehot, axis=0) * onehot, axis=1) - 1
    values = jnp.concatenate([mover_pos.reshape(2, -1), mover_strength.reshape(1, -1)])
    outgoing = (
        jnp.zeros((3, cell_count, CAP), jnp.float32).at[:, owner_cell, rank_in_owner].set(values)
    )
    addresses = (
        jnp.full((1, cell_count, CAP), half_slots * leaves, jnp.int32)
        .at[0, owner_cell, rank_in_owner]
        .set(address)
    )
    arrived, arrived_at = (
        lax.all_to_all(outgoing, "cell", split_axis=1, concat_axis=1, tiled=True),
        lax.all_to_all(addresses, "cell", split_axis=1, concat_axis=1, tiled=True),
    )
    resident = jnp.concatenate([resident_pos.reshape(2, -1), resident_strength.reshape(1, -1)])
    settled = resident.at[:, arrived_at.reshape(-1)].set(arrived.reshape(3, -1), mode="drop")
    return fields(settled.reshape(3, half_slots, cells_y, cells_x))


def solution(mesh):
    return jax.shard_map(
        local,
        mesh=mesh,
        in_specs=(
            P(None, "rep", "level", "cell"),
            P("rep", "level", "cell"),
            P(None, "rep", "level", "cell"),
            P("rep", "level", "cell"),
            P("rep", "level", "cell"),
            P("rep", "level", "cell"),
            P("rep", "level", "cell"),
        ),
        out_specs=P(None, "rep", "level", "cell"),
        check_vma=False,
    )
```

```python
import functools
import math

import jax
import jax.numpy as jnp
import numpy as np
from jax import lax
from jax.experimental import pallas as pl
from jax.experimental.pallas import tpu as pltpu
from jax.sharding import PartitionSpec as P

ORDER = 10
CHAN = 2 * ORDER
FAMILY = 4 * CHAN
CAP = 1024
BLOB = 0.09
LANES = 128
HEIGHTS = (16, 8, 4, 2, 1)
WIDTHS = (64, 32, 16, 8, 4)
OFFSETS = (0, 16, 24, 28, 30)
ROWS = 31
PACKS = (None, 0, 34, 52, 62)
VMEM = 56 * 2**20

f32 = jnp.float32
bf16 = jnp.bfloat16
precise = lax.Precision.HIGHEST


def real_form(matrix):
    top_rows = np.concatenate([matrix.real, -matrix.imag], axis=1)
    low_rows = np.concatenate([matrix.imag, matrix.real], axis=1)
    return np.concatenate([top_rows, low_rows], axis=0)


def child_offset(parity_x, parity_y):
    return complex((parity_x - 0.5) / 2.0, (parity_y - 0.5) / 2.0)


def upward_table(parity_x, parity_y):
    offset = child_offset(parity_x, parity_y)
    matrix = np.zeros((ORDER, ORDER), complex)
    for k in range(ORDER):
        for m in range(k + 1):
            matrix[k, m] = math.comb(k, m) * 0.5**m * offset ** (k - m)
    return real_form(matrix)


def downward_table(parity_x, parity_y):
    offset = child_offset(parity_x, parity_y)
    matrix = np.zeros((ORDER, ORDER), complex)
    for m in range(ORDER):
        for l in range(m, ORDER):
            matrix[m, l] = 0.5 ** (m + 1) * math.comb(l, m) * offset ** (l - m)
    return real_form(matrix)


def far_table(step_x, step_y):
    distance = complex(step_x, step_y)
    matrix = np.zeros((ORDER, ORDER), complex)
    for l in range(ORDER):
        for k in range(ORDER):
            matrix[l, k] = (-1) ** (k + 1) * math.comb(k + l, l) * distance ** (-(k + l + 1))
    return real_form(matrix)


def family(parity_x, parity_y):
    first = (2 * parity_x + parity_y) * CHAN
    return slice(first, first + CHAN)


def upward_family():
    table = np.zeros((CHAN, FAMILY))
    for b in (0, 1):
        for a in (0, 1):
            table[:, family(b, a)] = upward_table(b, a)
    return table


def downward_family():
    table = np.zeros((FAMILY, CHAN))
    for b in (0, 1):
        for a in (0, 1):
            table[family(b, a), :] = downward_table(b, a)
    return table


def far_family():
    table = np.zeros((3, FAMILY, 3, FAMILY))
    for dx in (-1, 0, 1):
        for dy in (-1, 0, 1):
            for bt in (0, 1):
                for at in (0, 1):
                    for bs in (0, 1):
                        for as_ in (0, 1):
                            step_x = 2 * dx + bs - bt
                            step_y = 2 * dy + as_ - at
                            if max(abs(step_x), abs(step_y)) >= 2:
                                table[dx + 1, family(bt, at), dy + 1, family(bs, as_)] = far_table(
                                    step_x, step_y
                                )
    return table.reshape(3 * FAMILY, 3 * FAMILY)


def coarse_tables():
    far5 = {}
    to_top = np.zeros((4, LANES, LANES))
    near5 = np.zeros((4, 12, LANES, LANES))
    from_top = np.zeros((4, LANES, LANES))
    lane = lambda column: np.arange(CHAN) * 4 + column
    for row in range(4):
        for column in range(4):
            lift = upward_table(column // 2, row // 2) @ upward_table(column % 2, row % 2)
            to_top[row][np.ix_(lane(column), np.arange(CHAN))] = lift.T
            drop = downward_table(column % 2, row % 2) @ downward_table(column // 2, row // 2)
            from_top[row][np.ix_(np.arange(CHAN), lane(column))] = drop.T
    for row in range(4):
        for column in range(4):
            down = downward_table(column % 2, row % 2)
            x = 4 + column
            for step in range(3):
                for other_row in range(4):
                    for other in range(4):
                        u = 4 * step + other
                        total = np.zeros((CHAN, CHAN))
                        if abs(u // 2 - x // 2) <= 1:
                            if max(abs(u - x), abs(other_row - row)) >= 2:
                                total += far_table(u - x, other_row - row)
                        if abs(u // 2 - x // 2) >= 2:
                            key = (u // 2 - x // 2, other_row // 2 - row // 2)
                            if key not in far5:
                                far5[key] = far_table(*key)
                            total += down @ far5[key] @ upward_table(other % 2, other_row % 2)
                        near5[row, step * 4 + other_row][np.ix_(lane(other), lane(column))] += total.T
    top = np.zeros((LANES, 32 * 32))
    for step in range(-15, 16):
        if abs(step) >= 2:
            top[:CHAN, (step + 15) * 32 : (step + 15) * 32 + CHAN] = far_table(step, 0).T
    return to_top, near5, from_top, top


def halves_np(table):
    high = np.asarray(table, np.float32).astype(jnp.bfloat16)
    low = (np.asarray(table, np.float32) - high.astype(np.float32)).astype(jnp.bfloat16)
    return high, low


def split_lanes():
    table = np.zeros((LANES, LANES), np.float32)
    x = np.arange(LANES)
    table[x, 64 * (x % 2) + x // 2] = 1.0
    return np.concatenate([table, table], axis=0).astype(jnp.bfloat16)


def join_lanes():
    table = np.zeros((2, LANES, LANES), np.float32)
    x = np.arange(64)
    table[0, x, 2 * x] = 1.0
    table[1, x, 2 * x + 1] = 1.0
    table = table.reshape(2 * LANES, LANES)
    return np.concatenate([table, table], axis=0).astype(jnp.bfloat16)


def quarter_lanes():
    k = np.arange(LANES)
    return (k[:, None] % 4 == k[None, :]).astype(np.float32)


def halves(value):
    high = value.astype(bf16)
    return high, (value - high.astype(f32)).astype(bf16)


def dot(left, right):
    return jnp.dot(left, right, preferred_element_type=f32)


def lane_index(rows):
    return lax.broadcasted_iota(jnp.int32, (rows, LANES), 1)


def whole(shape):
    return pl.BlockSpec(shape, lambda *_: (0,) * len(shape))


def upward_kernel(
    own, other, split_ref, lift_ref, spread_ref, cells, packed, coarse, mom, raw
):
    for tile in range(4):
        rows = pl.ds(8 * tile, 8)

        def add_slot(j, sums):
            for ref in (own, other):
                x, y, re = ref[0, j, rows, :], ref[1, j, rows, :], ref[2, j, rows, :]
                real, imag = list(sums[:ORDER]), list(sums[ORDER:])
                real[0] = real[0] + re
                im = re * y
                re = re * x
                real[1] = real[1] + re
                imag[1] = imag[1] + im
                for k in range(2, ORDER):
                    re, im = re * x - im * y, re * y + im * x
                    real[k] = real[k] + re
                    imag[k] = imag[k] + im
                sums = tuple(real + imag)
            return sums

        sums = lax.fori_loop(
            0, 16, add_slot, tuple(jnp.zeros((8, LANES), f32) for _ in range(CHAN)), unroll=2
        )
        for c in range(CHAN):
            mom[pl.ds(8 * tile * CHAN + c, 8, stride=CHAN), :] = sums[c]

    lane40 = lane_index(40)
    lane80 = lane_index(FAMILY)
    first = jnp.zeros((FAMILY, LANES), f32)
    last = jnp.zeros((FAMILY, LANES), f32)
    for k, height in enumerate(HEIGHTS):
        source = mom[...] if k == 0 else raw[pl.ds(0, 40 * height), :]
        spread = dot(jnp.concatenate(halves(source), axis=1), split_ref[...])
        parents = []
        for row in range(height):
            block = spread[40 * row : 40 * row + 40]
            even = jnp.where(lane40 < 64, block, 0.0)
            odd = jnp.where(lane40 < 64, pltpu.roll(block, 64, 1), 0.0)
            parent = jnp.concatenate([even, odd], axis=0)
            index = OFFSETS[k] + row
            cells[pl.ds(FAMILY * index, FAMILY), :] = parent
            first = jnp.where(lane80 == index, pltpu.roll(parent, index, 1), first)
            last = jnp.where(
                lane80 == index, pltpu.roll(parent, (index - WIDTHS[k] + 1) % LANES, 1), last
            )
            parents.append(parent)
        high, low = halves(jnp.concatenate(parents, axis=1))
        lifted = dot(lift_ref[...], jnp.concatenate([high, low, high], axis=0))
        for row in range(height):
            raw[pl.ds(CHAN * row, CHAN), :] = lifted[:CHAN, LANES * row : LANES * (row + 1)]
    packed[0, pl.ds(32, FAMILY), :] = first
    packed[1, pl.ds(32, FAMILY), :] = last

    four = jnp.dot(raw[pl.ds(0, 24), :], spread_ref[...], precision=precise)
    row24 = lax.broadcasted_iota(jnp.int32, (24, LANES), 0)
    line = jnp.sum(jnp.where((lane_index(24) // 4 == row24) & (row24 < CHAN), four, 0.0), axis=0, keepdims=True)
    coarse[...] = jnp.broadcast_to(line, coarse.shape)

    lane32 = lane_index(32)

    def edge(j, sides):
        left, right = sides
        for half, ref in enumerate((own, other)):
            for comp in range(3):
                m = comp * 32 + half * 16 + j
                value = ref[comp, j]
                left = jnp.where(lane32 == m, pltpu.roll(value, m, 1), left)
                right = jnp.where(lane32 == m, pltpu.roll(value, m + 1, 1), right)
        return left, right

    zero = jnp.zeros((32, LANES), f32)
    left, right = lax.fori_loop(0, 16, edge, (zero, zero))
    packed[0, pl.ds(0, 32), :] = left
    packed[1, pl.ds(0, 32), :] = right


def ring_columns(parent, k, index, from_left, from_right, lane):
    width = WIDTHS[k]
    parent = jnp.where(lane == LANES - 1, pltpu.roll(from_left, (LANES - 1 - index) % LANES, 1), parent)
    return jnp.where(lane == width, pltpu.roll(from_right, (width - index) % LANES, 1), parent)


def rows_kernel(own, other, cells, from_left, from_right, out):
    lane80 = lane_index(FAMILY)
    left, right = from_left[pl.ds(32, FAMILY), :], from_right[pl.ds(32, FAMILY), :]
    for side in (0, 1):
        row = 31 * side
        for comp in range(3):
            for half, ref in enumerate((own, other)):
                for j in range(16):
                    out[side, pl.ds(comp * 32 + half * 16 + j, 1), :] = ref[comp, j, pl.ds(row, 1), :]
        out[side, pl.ds(96, 1), :] = from_left[pl.ds(row, 1), :]
        out[side, pl.ds(97, 1), :] = from_right[pl.ds(row, 1), :]
        out[side, pl.ds(98, 6), :] = jnp.zeros((6, LANES), f32)
        packed = jnp.zeros((FAMILY, LANES), f32)
        for k, height in enumerate(HEIGHTS):
            index = OFFSETS[k] + (height - 1) * side
            parent = cells[pl.ds(FAMILY * index, FAMILY), :]
            parent = ring_columns(parent, k, index, left, right, lane80)
            if k == 0:
                out[side, pl.ds(104, FAMILY), :] = parent
            else:
                moved = pltpu.roll(parent, PACKS[k] + 1, 1)
                inside = (lane80 >= PACKS[k]) & (lane80 < PACKS[k] + WIDTHS[k] + 2)
                packed = jnp.where(inside, moved, packed)
        out[side, pl.ds(104 + FAMILY, FAMILY), :] = packed


GROUP = 8


def near_kernel(own, other, from_left, from_right, above, below, out, src):
    lane32 = lane_index(32)
    lane1 = lane_index(1)

    for comp in range(3):
        for half, ref in enumerate((own, other)):

            def frame(j, _, comp=comp, half=half, ref=ref):
                m = comp * 32 + half * 16 + j
                back = (LANES - m) % LANES if isinstance(m, int) else LANES - m
                value = ref[comp, j]
                rows = (value, above[pl.ds(m, 1), :], below[pl.ds(m, 1), :])
                lefts = (from_left[pl.ds(0, 32), :], above[pl.ds(96, 1), :], below[pl.ds(96, 1), :])
                rights = (from_right[pl.ds(0, 32), :], above[pl.ds(97, 1), :], below[pl.ds(97, 1), :])
                for part in range(3):
                    place = (pl.ds(8, 32), pl.ds(7, 1), pl.ds(40, 1))[part]
                    lane = lane32 if part == 0 else lane1
                    middle = rows[part]
                    before = jnp.where(
                        lane == 0, pltpu.roll(lefts[part], back, 1), pltpu.roll(middle, 1, 1)
                    )
                    after = jnp.where(
                        lane == LANES - 1,
                        pltpu.roll(rights[part], LANES - 1 - m, 1),
                        pltpu.roll(middle, LANES - 1, 1),
                    )
                    if comp == 0:
                        before = before - 1.0
                        after = after + 1.0
                    src[0, m, place, :] = before
                    src[1, m, place, :] = middle
                    src[2, m, place, :] = after
                return 0

            lax.fori_loop(0, 16, frame, 0)

    for tile in range(4):
        for group in range(16 // GROUP):
            tx = [own[0, group * GROUP + i, pl.ds(8 * tile, 8), :] for i in range(GROUP)]
            ty0 = [own[1, group * GROUP + i, pl.ds(8 * tile, 8), :] for i in range(GROUP)]
            acc = tuple(jnp.zeros((8, LANES), f32) for _ in range(2 * GROUP))
            for dy in (-1, 0, 1):
                ty = [value - float(dy) for value in ty0] if dy else ty0
                rows = pl.ds(8 + 8 * tile + dy, 8)
                for dx in range(3):

                    def pairs(j, acc, dx=dx, rows=rows, ty=ty, tx=tx):
                        acc = list(acc)
                        sx, sy, q = src[dx, j, rows, :], src[dx, 32 + j, rows, :], src[dx, 64 + j, rows, :]
                        for i in range(GROUP):
                            gap_x = tx[i] - sx
                            gap_y = ty[i] - sy
                            weight = q * (1.0 / (gap_x * gap_x + (gap_y * gap_y + BLOB)))
                            acc[i] = acc[i] + weight * gap_x
                            acc[GROUP + i] = acc[GROUP + i] + weight * gap_y
                        return tuple(acc)

                    acc = lax.fori_loop(0, 32, pairs, acc, unroll=4)
            for i in range(GROUP):
                out[0, group * GROUP + i, pl.ds(8 * tile, 8), :] = acc[i]
                out[1, group * GROUP + i, pl.ds(8 * tile, 8), :] = acc[GROUP + i]


def far_kernel(
    place, own, near, cells, from_left, from_right, above, below, gathered,
    far_ref, drop_ref, join_ref, spread_ref, to_top, near5, from_top, top_ref,
    out, high, low, fars, paired, joined_ref, loc,
):
    cell = place[0]
    level = place[1]
    tops = jnp.zeros((16, LANES), f32)
    for row in range(4):
        tops = tops + jnp.dot(gathered[pl.ds(row, 16, stride=4), :], to_top[row], precision=precise)
    spread = jnp.dot(tops, top_ref[...], precision=precise)
    source = lax.broadcasted_iota(jnp.int32, (16, 1024), 0)
    step = lax.broadcasted_iota(jnp.int32, (16, 1024), 1) // 32
    line = jnp.sum(jnp.where(step == source - cell + 15, spread, 0.0), axis=0, keepdims=True)
    total = line[:, :LANES]
    for block in range(1, 8):
        total = total + line[:, LANES * block : LANES * (block + 1)]
    total = jnp.broadcast_to(total, (8, LANES))
    total = total + pltpu.roll(total, 64, 1)
    total = total + pltpu.roll(total, 32, 1)
    total = jnp.where(lane_index(8) < CHAN, total, 0.0)
    five = jnp.dot(total, from_top[0], precision=precise)
    for step in range(3):
        there = cell + step - 1
        valid = jnp.where((there >= 0) & (there < 16), 1.0, 0.0)
        there = jnp.clip(there, 0, 15)
        for row in range(4):
            value = jnp.broadcast_to(gathered[pl.ds(there * 4 + row, 1), :], (8, LANES)) * valid
            five = five + jnp.dot(value, near5[0, step * 4 + row], precision=precise)
    five = jnp.broadcast_to(five[0:1], (32, LANES))
    row32 = lax.broadcasted_iota(jnp.int32, (32, LANES), 0)
    five = jnp.where((lane_index(32) // 4 == row32) & (row32 < CHAN), five, 0.0)
    loc[...] = jnp.zeros(loc.shape, f32)
    loc[pl.ds(0, 32), pl.ds(0, LANES)] = jnp.dot(five, spread_ref[...], precision=precise)

    lane80 = lane_index(FAMILY)
    left, right = from_left[pl.ds(32, FAMILY), :], from_right[pl.ds(32, FAMILY), :]
    start = 0
    starts = []
    for k, height in enumerate(HEIGHTS):
        starts.append(start)
        for row in range(-1, height + 1):
            if row in (-1, height):
                ref = above if row == -1 else below
                if k == 0:
                    parent = ref[pl.ds(104, FAMILY), :]
                else:
                    packed = ref[pl.ds(104 + FAMILY, FAMILY), :]
                    parent = pltpu.roll(packed, LANES - PACKS[k] - 1, 1)
                    parent = jnp.where((lane80 <= WIDTHS[k]) | (lane80 == LANES - 1), parent, 0.0)
            else:
                index = OFFSETS[k] + row
                parent = cells[pl.ds(FAMILY * index, FAMILY), :]
                parent = ring_columns(parent, k, index, left, right, lane80)
            part_high, part_low = halves(parent)
            high[pl.ds(FAMILY * start, FAMILY), :] = part_high
            low[pl.ds(FAMILY * start, FAMILY), :] = part_low
            start += 1

    def far_rows(k, rows):
        both = []
        for ref in (high, low):
            both.append(
                jnp.concatenate(
                    [ref[pl.ds(FAMILY * (starts[k] + row), 3 * FAMILY), :] for row in rows], axis=1
                )
            )
        size = 3 * FAMILY
        product = dot(far_ref[...], both[0])
        product = product[:size] + product[size:] + dot(far_ref[pl.ds(0, size), :], both[1])
        for place_, row in enumerate(rows):
            part = product[:, LANES * place_ : LANES * (place_ + 1)]
            fars[pl.ds(FAMILY * (OFFSETS[k] + row), FAMILY), :] = (
                part[FAMILY : 2 * FAMILY]
                + pltpu.roll(part[:FAMILY], 1, 1)
                + pltpu.roll(part[2 * FAMILY :], LANES - 1, 1)
            )

    for k, height in enumerate(HEIGHTS):
        for row in range(0, height, 2):
            far_rows(k, (row, row + 1) if height > 1 else (row,))

    for k in range(4, -1, -1):
        height = HEIGHTS[k]
        part_high, part_low = halves(loc[:, pl.ds(0, LANES * height)])
        dropped = dot(drop_ref[...], jnp.concatenate([part_high, part_low, part_high], axis=0))
        for row in range(height):
            here = dropped[:, LANES * row : LANES * (row + 1)] + fars[pl.ds(FAMILY * (OFFSETS[k] + row), FAMILY), :]
            paired[pl.ds(40 * row, 40), :] = jnp.concatenate([here[:40], here[40:]], axis=1)
        part_high, part_low = halves(paired[pl.ds(0, 40 * height), :])
        joined = dot(jnp.concatenate([part_high, part_low], axis=1), join_ref[...])
        joined_ref[pl.ds(0, 40 * height), :] = joined
        if k > 0:
            for row in range(2 * height):
                loc[pl.ds(0, CHAN), pl.ds(LANES * row, LANES)] = joined_ref[pl.ds(CHAN * row, CHAN), :]

    scale = 1.0 / (2.0 * math.pi)
    for tile in range(4):
        rows = pl.ds(8 * tile, 8)
        terms = [joined_ref[pl.ds(8 * tile * CHAN + c, 8, stride=CHAN), :] for c in range(CHAN)]

        def value(j, _, terms=terms, rows=rows):
            x, y = own[0, j, rows, :], own[1, j, rows, :]
            re, im = terms[ORDER - 1], terms[CHAN - 1]
            for l in range(ORDER - 2, -1, -1):
                re, im = re * x - im * y + terms[l], re * y + im * x + terms[ORDER + l]
            out[0, j, rows, :] = (im - near[1, j, rows, :]) * scale
            out[1, j, rows, :] = (re + near[0, j, rows, :]) * scale
            return 0

        lax.fori_loop(0, 16, value, 0, unroll=2)


def params():
    return pltpu.CompilerParams(vmem_limit_bytes=VMEM)


def shape(*sizes):
    return jax.ShapeDtypeStruct(sizes, f32)


def neighbours(value, axis, step):
    size = lax.axis_size(axis)
    return lax.ppermute(value, axis, [(i, i + step) for i in range(size) if 0 <= i + step < size])


def fields(own):
    other = lax.ppermute(own, "rep", [(0, 1), (1, 0)])
    lift_high, lift_low = halves_np(upward_family())
    lift = np.zeros((32, 3 * FAMILY), jnp.bfloat16)
    lift[:CHAN] = np.concatenate([lift_high, lift_high, lift_low], axis=1)
    cells, packed, coarse = pl.pallas_call(
        upward_kernel,
        out_shape=(shape(ROWS * FAMILY, LANES), shape(2, 32 + FAMILY, LANES), shape(64, LANES)),
        scratch_shapes=[pltpu.VMEM((640, LANES), f32), pltpu.VMEM((320, LANES), f32)],
        compiler_params=params(),
        name="upward",
    )(own, other, jnp.asarray(split_lanes()), jnp.asarray(lift), jnp.asarray(quarter_lanes().T.copy()))
    from_left = neighbours(packed[1], "cell", 1)
    from_right = neighbours(packed[0], "cell", -1)
    gathered = lax.all_to_all(coarse, ("cell", "level"), 0, 0, tiled=True)
    rows = pl.pallas_call(
        rows_kernel,
        out_shape=shape(2, 104 + 2 * FAMILY, LANES),
        compiler_params=params(),
        name="rows",
    )(own, other, cells, from_left, from_right)
    above = neighbours(rows[1], "level", 1)
    below = neighbours(rows[0], "level", -1)
    near = pl.pallas_call(
        near_kernel,
        out_shape=shape(2, 16, 32, LANES),
        scratch_shapes=[pltpu.VMEM((3, 96, 48, LANES), f32)],
        compiler_params=params(),
        name="near",
    )(own, other, from_left, from_right, above, below)
    far_high, far_low = halves_np(far_family())
    drop_table = np.zeros((FAMILY, 32))
    drop_table[:, :CHAN] = downward_family()
    drop_high, drop_low = halves_np(drop_table)
    to_top, near5, from_top, top = coarse_tables()
    tables = [
        np.concatenate([far_high, far_low], axis=0),
        np.concatenate([drop_high, drop_high, drop_low], axis=1),
        join_lanes(),
        quarter_lanes(),
        to_top.astype(np.float32),
        near5.astype(np.float32),
        from_top.astype(np.float32),
        top.astype(np.float32),
    ]
    operands = [own, near, cells, from_left, from_right, above, below, gathered] + [
        jnp.asarray(table) for table in tables
    ]
    specs = [whole(value.shape) for value in operands]
    specs[13] = pl.BlockSpec((1, 12, LANES, LANES), lambda i, place: (place[1], 0, 0, 0))
    specs[14] = pl.BlockSpec((1, LANES, LANES), lambda i, place: (place[1], 0, 0))
    place = jnp.stack([lax.axis_index("cell"), lax.axis_index("level")]).astype(jnp.int32)
    return pl.pallas_call(
        far_kernel,
        grid_spec=pltpu.PrefetchScalarGridSpec(
            num_scalar_prefetch=1,
            grid=(1,),
            in_specs=specs,
            out_specs=whole((2, 16, 32, LANES)),
            scratch_shapes=[
                pltpu.VMEM((41 * FAMILY, LANES), bf16),
                pltpu.VMEM((41 * FAMILY, LANES), bf16),
                pltpu.VMEM((ROWS * FAMILY, LANES), f32),
                pltpu.VMEM((640, 2 * LANES), f32),
                pltpu.VMEM((640, LANES), f32),
                pltpu.VMEM((32, 16 * LANES), f32),
            ],
        ),
        out_shape=shape(2, 16, 32, LANES),
        compiler_params=params(),
        name="far",
    )(place, *operands)


def flat_index(shape_):
    rows = lax.broadcasted_iota(jnp.int32, shape_, 0)
    return rows * LANES + lax.broadcasted_iota(jnp.int32, shape_, 1)


def exchange(key, loads, index, distance, descending):
    high = (index & distance) != 0
    axis = 1 if distance < LANES else 0
    step = distance if axis else distance // LANES
    size = key.shape[axis]

    def partner(value):
        down = pltpu.roll(value, step, axis)
        if 2 * step == size:
            return down
        return jnp.where(high, down, pltpu.roll(value, size - step, axis))

    flip = high if descending is None else high ^ descending
    other = partner(key)
    take = (other < key) ^ flip
    return jnp.where(take, other, key), [jnp.where(take, partner(load), load) for load in loads]


def pack_kernel(odd_ref, pos, strength, owner_ref, leaf, slot, out, keys, values):
    odd = odd_ref[0]
    owner = owner_ref[...]
    address = slot[...] * 4096 + leaf[...]
    address = jnp.where(odd == 1, 65535 - address, address)
    key = owner * 65536 + address
    loads = [pos[0], pos[1], strength[...]]
    index = flat_index((32, LANES))
    for block in range(1, 13):
        descending = None if block == 12 else (index & (1 << block)) != 0
        for bit in range(block - 1, -1, -1):
            key, loads = exchange(key, loads, index, 1 << bit, descending)
    keys[...] = jnp.full(keys.shape, -1, jnp.int32)
    keys[pl.ds(8, 32), :] = key
    for c in range(3):
        values[c, pl.ds(8, 32), :] = loads[c]
    lane = lane_index(8)
    for o in range(16):
        bound = jnp.where(odd == 1, o + 1, o)
        start = jnp.sum((owner < bound).astype(jnp.int32)) + jnp.where(odd == 1, 0, 1024)
        row = start // LANES
        shift = start % LANES
        back = jnp.where(shift == 0, 0, LANES - shift)

        def window(ref):
            upper = pltpu.roll(ref[pl.ds(row, 8), :], back, 1)
            lower = pltpu.roll(ref[pl.ds(row + 1, 8), :], back, 1)
            return jnp.where(lane < LANES - shift, upper, lower)

        mine = window(keys)
        place = mine - o * 65536
        valid = (place >= 0) & (place < 65536)
        place = jnp.where(odd == 1, 65535 - place, place)
        out[o, 3] = jnp.where(valid, place, 65536).astype(f32)
        for c in range(3):
            out[o, c] = window(values.at[c])


def settle_kernel(arrived, pos, strength, out, marks_a, marks_b, loads_a, loads_b):
    index = flat_index((LANES, LANES))
    key = arrived[:, 3].reshape(LANES, LANES)
    loads = [arrived[:, c].reshape(LANES, LANES) for c in range(3)]
    for block in range(11, 15):
        descending = None if block == 14 else (index & (1 << block)) != 0
        for bit in range(block - 1, -1, -1):
            key, loads = exchange(key, loads, index, 1 << bit, descending)
    address = key.astype(jnp.int32)
    mark = jnp.where(address < 65536, 2 * (address - index) + 1, 0)
    size = 576
    for ref in (marks_a, marks_b):
        ref[...] = jnp.zeros((size, LANES), jnp.int32)
    marks_a[pl.ds(64, LANES), :] = mark
    for c in range(3):
        loads_a[c, pl.ds(64, LANES), :] = loads[c]
    lane = lane_index(64)
    marks, values = (marks_a, marks_b), (loads_a, loads_b)
    for bit in range(15, -1, -1):
        now, later = marks[bit % 2 == 0], marks[bit % 2]
        load_now, load_later = values[bit % 2 == 0], values[bit % 2]
        test = 2 << bit
        rows = (1 << bit) // LANES

        def step(block, _, now=now, later=later, load_now=load_now, load_later=load_later, test=test, rows=rows, bit=bit):
            base = pl.multiple_of(block * 64, 64)
            here = pl.ds(base + 64, 64)

            def source(ref):
                if rows:
                    if rows >= 64:
                        start = pl.multiple_of(jnp.maximum(base + 64 - rows, 0), 8)
                        return ref[pl.ds(start, 64), :]
                    return ref[pl.ds(base + 64 - rows, 64), :]
                near = pltpu.roll(ref[here, :], 1 << bit, 1)
                before = pltpu.roll(ref[pl.ds(base + 63, 64), :], 1 << bit, 1)
                return jnp.where(lane < (1 << bit), before, near)

            own = now[here, :]
            own = jnp.where((own & test) != 0, 0, own)
            there = source(now)
            come = (there & test) != 0
            if rows >= 64:
                come = come & (base >= rows)
            later[here, :] = jnp.where(come, there, own)
            for c in range(3):
                load_later[c, here, :] = jnp.where(come, source(load_now.at[c]), load_now[c, here, :])
            return 0

        lax.fori_loop(0, 8, step, 0)
    for j in range(16):
        rows = pl.ds(64 + 32 * j, 32)
        moved = marks_a[rows, :] != 0
        out[0, j] = jnp.where(moved, loads_a[0, rows, :], pos[0, j])
        out[1, j] = jnp.where(moved, loads_a[1, rows, :], pos[1, j])
        out[2, j] = jnp.where(moved, loads_a[2, rows, :], strength[j])


def local(
    resident_pos, resident_strength, mover_pos, mover_strength, mover_owner, mover_leaf, mover_slot
):
    smem = pl.BlockSpec(memory_space=pltpu.SMEM)
    vmem = pl.BlockSpec(memory_space=pltpu.VMEM)
    odd = (lax.axis_index("cell") % 2).astype(jnp.int32).reshape(1)
    outgoing = pl.pallas_call(
        pack_kernel,
        in_specs=[smem] + [vmem] * 5,
        out_shape=shape(16, 4, 8, LANES),
        scratch_shapes=[pltpu.VMEM((56, LANES), jnp.int32), pltpu.VMEM((3, 56, LANES), f32)],
        compiler_params=params(),
        name="pack",
    )(
        odd,
        mover_pos.reshape(2, 32, LANES),
        mover_strength.reshape(32, LANES),
        mover_owner.reshape(32, LANES),
        mover_leaf.reshape(32, LANES),
        mover_slot.reshape(32, LANES),
    )
    arrived = lax.all_to_all(outgoing, "cell", 0, 0, tiled=True)
    own = pl.pallas_call(
        settle_kernel,
        out_shape=shape(3, 16, 32, LANES),
        scratch_shapes=[
            pltpu.VMEM((576, LANES), jnp.int32),
            pltpu.VMEM((576, LANES), jnp.int32),
            pltpu.VMEM((3, 576, LANES), f32),
            pltpu.VMEM((3, 576, LANES), f32),
        ],
        compiler_params=params(),
        name="settle",
    )(arrived, resident_pos, resident_strength)
    return fields(own)


def solution(mesh):
    return jax.shard_map(
        local,
        mesh=mesh,
        in_specs=(
            P(None, "rep", "level", "cell"),
            P("rep", "level", "cell"),
            P(None, "rep", "level", "cell"),
            P("rep", "level", "cell"),
            P("rep", "level", "cell"),
            P("rep", "level", "cell"),
            P("rep", "level", "cell"),
        ),
        out_specs=P(None, "rep", "level", "cell"),
        check_vma=False,
    )
```

```python
import functools
import math

import jax
import jax.numpy as jnp
import numpy as np
from jax import lax
from jax.experimental import pallas as pl
from jax.experimental.pallas import tpu as pltpu
from jax.sharding import PartitionSpec as P

ORDER = 10
CHAN = 2 * ORDER
FAMILY = 4 * CHAN
CAP = 1024
BLOB = 0.09
LANES = 128
HEIGHTS = (16, 8, 4, 2, 1)
WIDTHS = (64, 32, 16, 8, 4)
OFFSETS = (0, 16, 24, 28, 30)
ROWS = 31
PACKS = (None, 0, 34, 52, 62)
VMEM = 56 * 2**20

f32 = jnp.float32
bf16 = jnp.bfloat16
precise = lax.Precision.HIGHEST


def real_form(matrix):
    top_rows = np.concatenate([matrix.real, -matrix.imag], axis=1)
    low_rows = np.concatenate([matrix.imag, matrix.real], axis=1)
    return np.concatenate([top_rows, low_rows], axis=0)


def child_offset(parity_x, parity_y):
    return complex((parity_x - 0.5) / 2.0, (parity_y - 0.5) / 2.0)


def upward_table(parity_x, parity_y):
    offset = child_offset(parity_x, parity_y)
    matrix = np.zeros((ORDER, ORDER), complex)
    for k in range(ORDER):
        for m in range(k + 1):
            matrix[k, m] = math.comb(k, m) * 0.5**m * offset ** (k - m)
    return real_form(matrix)


def downward_table(parity_x, parity_y):
    offset = child_offset(parity_x, parity_y)
    matrix = np.zeros((ORDER, ORDER), complex)
    for m in range(ORDER):
        for l in range(m, ORDER):
            matrix[m, l] = 0.5 ** (m + 1) * math.comb(l, m) * offset ** (l - m)
    return real_form(matrix)


def far_table(step_x, step_y):
    distance = complex(step_x, step_y)
    matrix = np.zeros((ORDER, ORDER), complex)
    for l in range(ORDER):
        for k in range(ORDER):
            matrix[l, k] = (-1) ** (k + 1) * math.comb(k + l, l) * distance ** (-(k + l + 1))
    return real_form(matrix)


def family(parity_x, parity_y):
    first = (2 * parity_x + parity_y) * CHAN
    return slice(first, first + CHAN)


def upward_family():
    table = np.zeros((CHAN, FAMILY))
    for b in (0, 1):
        for a in (0, 1):
            table[:, family(b, a)] = upward_table(b, a)
    return table


def downward_family():
    table = np.zeros((FAMILY, CHAN))
    for b in (0, 1):
        for a in (0, 1):
            table[family(b, a), :] = downward_table(b, a)
    return table


def far_family():
    table = np.zeros((3, FAMILY, 3, FAMILY))
    for dx in (-1, 0, 1):
        for dy in (-1, 0, 1):
            for bt in (0, 1):
                for at in (0, 1):
                    for bs in (0, 1):
                        for as_ in (0, 1):
                            step_x = 2 * dx + bs - bt
                            step_y = 2 * dy + as_ - at
                            if max(abs(step_x), abs(step_y)) >= 2:
                                table[dx + 1, family(bt, at), dy + 1, family(bs, as_)] = far_table(
                                    step_x, step_y
                                )
    return table.reshape(3 * FAMILY, 3 * FAMILY)


def coarse_tables():
    far5 = {}
    to_top = np.zeros((4, LANES, LANES))
    near5 = np.zeros((4, 12, LANES, LANES))
    from_top = np.zeros((4, LANES, LANES))
    lane = lambda column: np.arange(CHAN) * 4 + column
    for row in range(4):
        for column in range(4):
            lift = upward_table(column // 2, row // 2) @ upward_table(column % 2, row % 2)
            to_top[row][np.ix_(lane(column), np.arange(CHAN))] = lift.T
            drop = downward_table(column % 2, row % 2) @ downward_table(column // 2, row // 2)
            from_top[row][np.ix_(np.arange(CHAN), lane(column))] = drop.T
    for row in range(4):
        for column in range(4):
            down = downward_table(column % 2, row % 2)
            x = 4 + column
            for step in range(3):
                for other_row in range(4):
                    for other in range(4):
                        u = 4 * step + other
                        total = np.zeros((CHAN, CHAN))
                        if abs(u // 2 - x // 2) <= 1:
                            if max(abs(u - x), abs(other_row - row)) >= 2:
                                total += far_table(u - x, other_row - row)
                        if abs(u // 2 - x // 2) >= 2:
                            key = (u // 2 - x // 2, other_row // 2 - row // 2)
                            if key not in far5:
                                far5[key] = far_table(*key)
                            total += down @ far5[key] @ upward_table(other % 2, other_row % 2)
                        near5[row, step * 4 + other_row][np.ix_(lane(other), lane(column))] += total.T
    top = np.zeros((LANES, 32 * 32))
    for step in range(-15, 16):
        if abs(step) >= 2:
            top[:CHAN, (step + 15) * 32 : (step + 15) * 32 + CHAN] = far_table(step, 0).T
    return to_top, near5, from_top, top


def halves_np(table):
    high = np.asarray(table, np.float32).astype(jnp.bfloat16)
    low = (np.asarray(table, np.float32) - high.astype(np.float32)).astype(jnp.bfloat16)
    return high, low


def split_lanes():
    table = np.zeros((LANES, LANES), np.float32)
    x = np.arange(LANES)
    table[x, 64 * (x % 2) + x // 2] = 1.0
    return np.concatenate([table, table], axis=0).astype(jnp.bfloat16)


def join_lanes():
    table = np.zeros((2, LANES, LANES), np.float32)
    x = np.arange(64)
    table[0, x, 2 * x] = 1.0
    table[1, x, 2 * x + 1] = 1.0
    table = table.reshape(2 * LANES, LANES)
    return np.concatenate([table, table], axis=0).astype(jnp.bfloat16)


def quarter_lanes():
    k = np.arange(LANES)
    return (k[:, None] % 4 == k[None, :]).astype(np.float32)


def halves(value):
    high = value.astype(bf16)
    return high, (value - high.astype(f32)).astype(bf16)


def dot(left, right):
    return jnp.dot(left, right, preferred_element_type=f32)


def lane_index(rows):
    return lax.broadcasted_iota(jnp.int32, (rows, LANES), 1)


def whole(shape):
    return pl.BlockSpec(shape, lambda *_: (0,) * len(shape))


def upward_kernel(
    own, other, split_ref, lift_ref, spread_ref, cells, packed, coarse, mom, raw
):
    for tile in range(4):
        rows = pl.ds(8 * tile, 8)

        def add_slot(j, sums):
            for ref in (own, other):
                x, y, re = ref[0, j, rows, :], ref[1, j, rows, :], ref[2, j, rows, :]
                real, imag = list(sums[:ORDER]), list(sums[ORDER:])
                real[0] = real[0] + re
                im = re * y
                re = re * x
                real[1] = real[1] + re
                imag[1] = imag[1] + im
                for k in range(2, ORDER):
                    re, im = re * x - im * y, re * y + im * x
                    real[k] = real[k] + re
                    imag[k] = imag[k] + im
                sums = tuple(real + imag)
            return sums

        sums = lax.fori_loop(
            0, 16, add_slot, tuple(jnp.zeros((8, LANES), f32) for _ in range(CHAN)), unroll=2
        )
        for c in range(CHAN):
            mom[pl.ds(8 * tile * CHAN + c, 8, stride=CHAN), :] = sums[c]

    lane40 = lane_index(40)
    lane80 = lane_index(FAMILY)
    first = jnp.zeros((FAMILY, LANES), f32)
    last = jnp.zeros((FAMILY, LANES), f32)
    for k, height in enumerate(HEIGHTS):
        source = mom[...] if k == 0 else raw[pl.ds(0, 40 * height), :]
        spread = dot(jnp.concatenate(halves(source), axis=1), split_ref[...])
        parents = []
        for row in range(height):
            block = spread[40 * row : 40 * row + 40]
            even = jnp.where(lane40 < 64, block, 0.0)
            odd = jnp.where(lane40 < 64, pltpu.roll(block, 64, 1), 0.0)
            parent = jnp.concatenate([even, odd], axis=0)
            index = OFFSETS[k] + row
            cells[pl.ds(FAMILY * index, FAMILY), :] = parent
            first = jnp.where(lane80 == index, pltpu.roll(parent, index, 1), first)
            last = jnp.where(
                lane80 == index, pltpu.roll(parent, (index - WIDTHS[k] + 1) % LANES, 1), last
            )
            parents.append(parent)
        high, low = halves(jnp.concatenate(parents, axis=1))
        lifted = dot(lift_ref[...], jnp.concatenate([high, low, high], axis=0))
        for row in range(height):
            raw[pl.ds(CHAN * row, CHAN), :] = lifted[:CHAN, LANES * row : LANES * (row + 1)]
    packed[0, pl.ds(32, FAMILY), :] = first
    packed[1, pl.ds(32, FAMILY), :] = last

    four = jnp.dot(raw[pl.ds(0, 24), :], spread_ref[...], precision=precise)
    row24 = lax.broadcasted_iota(jnp.int32, (24, LANES), 0)
    line = jnp.sum(jnp.where((lane_index(24) // 4 == row24) & (row24 < CHAN), four, 0.0), axis=0, keepdims=True)
    coarse[...] = jnp.broadcast_to(line, coarse.shape)

    lane32 = lane_index(32)

    left = right = jnp.zeros((32, LANES), f32)
    for half, ref in enumerate((own, other)):
        for comp in range(3):
            for j in range(16):
                m = comp * 32 + half * 16 + j
                value = ref[comp, j]
                left = jnp.where(lane32 == m, pltpu.roll(value, m, 1), left)
                right = jnp.where(lane32 == m, pltpu.roll(value, m + 1, 1), right)
    packed[0, pl.ds(0, 32), :] = left
    packed[1, pl.ds(0, 32), :] = right


def ring_columns(parent, k, index, from_left, from_right, lane):
    width = WIDTHS[k]
    parent = jnp.where(lane == LANES - 1, pltpu.roll(from_left, (LANES - 1 - index) % LANES, 1), parent)
    return jnp.where(lane == width, pltpu.roll(from_right, (width - index) % LANES, 1), parent)


def rows_kernel(place, own, other, cells, came_left, came_right, out, from_left, from_right):
    lane80 = lane_index(FAMILY)
    from_left[...] = jnp.where(place[0] > 0, came_left[...], 0.0)
    from_right[...] = jnp.where(place[0] < 15, came_right[...], 0.0)
    left, right = from_left[pl.ds(32, FAMILY), :], from_right[pl.ds(32, FAMILY), :]
    for side in (0, 1):
        row = 31 * side
        for comp in range(3):
            for half, ref in enumerate((own, other)):
                for j in range(16):
                    out[side, pl.ds(comp * 32 + half * 16 + j, 1), :] = ref[comp, j, pl.ds(row, 1), :]
        out[side, pl.ds(96, 1), :] = from_left[pl.ds(row, 1), :]
        out[side, pl.ds(97, 1), :] = from_right[pl.ds(row, 1), :]
        out[side, pl.ds(98, 6), :] = jnp.zeros((6, LANES), f32)
        packed = jnp.zeros((FAMILY, LANES), f32)
        for k, height in enumerate(HEIGHTS):
            index = OFFSETS[k] + (height - 1) * side
            parent = cells[pl.ds(FAMILY * index, FAMILY), :]
            parent = ring_columns(parent, k, index, left, right, lane80)
            if k == 0:
                out[side, pl.ds(104, FAMILY), :] = parent
            else:
                moved = pltpu.roll(parent, PACKS[k] + 1, 1)
                inside = (lane80 >= PACKS[k]) & (lane80 < PACKS[k] + WIDTHS[k] + 2)
                packed = jnp.where(inside, moved, packed)
        out[side, pl.ds(104 + FAMILY, FAMILY), :] = packed


GROUP = 8


def near_kernel(place, own, other, from_left, from_right, came_above, came_below, out, src, above, below):
    above[...] = jnp.where(place[1] > 0, came_above[pl.ds(0, 104), :], 0.0)
    below[...] = jnp.where(place[1] < 3, came_below[pl.ds(0, 104), :], 0.0)
    lane32 = lane_index(32)
    lane1 = lane_index(1)

    for comp in range(3):
        for half, ref in enumerate((own, other)):
            for j in range(16):
                m = comp * 32 + half * 16 + j
                rows = (ref[comp, j], above[pl.ds(m, 1), :], below[pl.ds(m, 1), :])
                lefts = (from_left[pl.ds(0, 32), :], above[pl.ds(96, 1), :], below[pl.ds(96, 1), :])
                rights = (from_right[pl.ds(0, 32), :], above[pl.ds(97, 1), :], below[pl.ds(97, 1), :])
                for part in range(3):
                    place = (pl.ds(8, 32), pl.ds(7, 1), pl.ds(40, 1))[part]
                    lane = lane32 if part == 0 else lane1
                    middle = rows[part]
                    before = pltpu.roll(middle, 1, 1)
                    after = pltpu.roll(middle, LANES - 1, 1)
                    left = pltpu.roll(lefts[part], (LANES - m) % LANES, 1)
                    right = pltpu.roll(rights[part], (LANES - 1 - m) % LANES, 1)
                    before = jnp.where(lane == 0, left, before)
                    after = jnp.where(lane == LANES - 1, right, after)
                    if comp == 0:
                        before = before - 1.0
                        after = after + 1.0
                    src[0, m, place, :] = before
                    src[1, m, place, :] = middle
                    src[2, m, place, :] = after

    for tile in range(4):
        for group in range(16 // GROUP):
            tx = [own[0, group * GROUP + i, pl.ds(8 * tile, 8), :] for i in range(GROUP)]
            ty0 = [own[1, group * GROUP + i, pl.ds(8 * tile, 8), :] for i in range(GROUP)]
            acc = tuple(jnp.zeros((8, LANES), f32) for _ in range(2 * GROUP))
            for dy in (-1, 0, 1):
                ty = [value - float(dy) for value in ty0] if dy else ty0
                rows = pl.ds(8 + 8 * tile + dy, 8)
                for dx in range(3):

                    def pairs(j, acc, dx=dx, rows=rows, ty=ty, tx=tx):
                        acc = list(acc)
                        sx, sy, q = src[dx, j, rows, :], src[dx, 32 + j, rows, :], src[dx, 64 + j, rows, :]
                        for i in range(GROUP):
                            gap_x = tx[i] - sx
                            gap_y = ty[i] - sy
                            weight = q * (1.0 / (gap_x * gap_x + (gap_y * gap_y + BLOB)))
                            acc[i] = acc[i] + weight * gap_x
                            acc[GROUP + i] = acc[GROUP + i] + weight * gap_y
                        return tuple(acc)

                    acc = lax.fori_loop(0, 32, pairs, acc, unroll=8)
            for i in range(GROUP):
                out[0, group * GROUP + i, pl.ds(8 * tile, 8), :] = acc[i]
                out[1, group * GROUP + i, pl.ds(8 * tile, 8), :] = acc[GROUP + i]


def three_products(value, table):
    product = dot(jnp.concatenate(halves(value), axis=0), table)
    return product[:16, :LANES] + product[16:, :LANES] + product[:16, LANES:]


def packed_parts(value):
    high = value.astype(bf16).astype(f32)
    low = value - high
    return (high + pltpu.roll(low, 32, 1) + pltpu.roll(high, 64, 1)).astype(bf16)


def side_by_side(table):
    return np.concatenate(halves_np(table), axis=-1)


def packed_table(table):
    high, low = halves_np(table)
    out = np.zeros(table.shape, jnp.bfloat16)
    out[..., 0:32, :] = high[..., 0:32, :]
    out[..., 32:64, :] = high[..., 0:32, :]
    out[..., 64:96, :] = low[..., 0:32, :]
    return out


def far_kernel(
    place, own, near, cells, from_left, from_right, above, below, gathered,
    far_ref, drop_ref, join_ref, spread_ref, to_top, near5, from_top, top_ref,
    out, high, low, fars, paired, joined_ref, loc,
):
    cell = place[0]
    level = place[1]
    tops = three_products(
        jnp.concatenate([gathered[pl.ds(row, 16, stride=4), :] for row in range(4)], axis=1), to_top[...]
    )
    spread = dot(packed_parts(tops), top_ref[...])
    source = lax.broadcasted_iota(jnp.int32, (16, 1024), 0)
    step = lax.broadcasted_iota(jnp.int32, (16, 1024), 1) // 32
    line = jnp.sum(jnp.where(step == source - cell + 15, spread, 0.0), axis=0, keepdims=True)
    total = line[:, :LANES]
    for block in range(1, 8):
        total = total + line[:, LANES * block : LANES * (block + 1)]
    total = jnp.broadcast_to(total, (16, LANES))
    total = total + pltpu.roll(total, 64, 1)
    total = total + pltpu.roll(total, 32, 1)
    total = jnp.where(lane_index(16) < CHAN, total, 0.0)
    around = []
    for step in range(3):
        there = cell + step - 1
        inside = (there >= 0) & (there < 16)
        there = jnp.clip(there, 0, 15)
        for row in range(4):
            value = gathered[pl.ds(there * 4 + row, 1), :]
            around.append(jnp.broadcast_to(jnp.where(inside, value, 0.0), (16, LANES)))
    five = dot(packed_parts(total), from_top[0]) + three_products(
        jnp.concatenate(around, axis=1), near5[0]
    )
    five = jnp.broadcast_to(five[0:1], (32, LANES))
    row32 = lax.broadcasted_iota(jnp.int32, (32, LANES), 0)
    five = jnp.where((lane_index(32) // 4 == row32) & (row32 < CHAN), five, 0.0)
    loc[...] = jnp.zeros(loc.shape, f32)
    loc[pl.ds(0, 32), pl.ds(0, LANES)] = dot(
        jnp.concatenate(halves(five), axis=1), spread_ref[...]
    )

    lane80 = lane_index(FAMILY)
    left, right = from_left[pl.ds(32, FAMILY), :], from_right[pl.ds(32, FAMILY), :]
    start = 0
    starts = []
    for k, height in enumerate(HEIGHTS):
        starts.append(start)
        for row in range(-1, height + 1):
            if row in (-1, height):
                ref = above if row == -1 else below
                inside = level > 0 if row == -1 else level < 3
                if k == 0:
                    parent = ref[pl.ds(104, FAMILY), :]
                else:
                    packed = ref[pl.ds(104 + FAMILY, FAMILY), :]
                    parent = pltpu.roll(packed, LANES - PACKS[k] - 1, 1)
                    parent = jnp.where((lane80 <= WIDTHS[k]) | (lane80 == LANES - 1), parent, 0.0)
            else:
                index = OFFSETS[k] + row
                parent = cells[pl.ds(FAMILY * index, FAMILY), :]
                parent = ring_columns(parent, k, index, left, right, lane80)
            if row in (-1, height):
                parent = jnp.where(inside, parent, 0.0)
            part_high, part_low = halves(parent)
            high[pl.ds(FAMILY * start, FAMILY), :] = part_high
            low[pl.ds(FAMILY * start, FAMILY), :] = part_low
            start += 1

    def far_rows(k, rows):
        both = []
        for ref in (high, low):
            both.append(
                jnp.concatenate(
                    [ref[pl.ds(FAMILY * (starts[k] + row), 3 * FAMILY), :] for row in rows], axis=1
                )
            )
        size = 3 * FAMILY
        product = dot(far_ref[...], both[0])
        product = product[:size] + product[size:] + dot(far_ref[pl.ds(0, size), :], both[1])
        for place_, row in enumerate(rows):
            part = product[:, LANES * place_ : LANES * (place_ + 1)]
            fars[pl.ds(FAMILY * (OFFSETS[k] + row), FAMILY), :] = (
                part[FAMILY : 2 * FAMILY]
                + pltpu.roll(part[:FAMILY], 1, 1)
                + pltpu.roll(part[2 * FAMILY :], LANES - 1, 1)
            )

    for k, height in enumerate(HEIGHTS):
        for row in range(0, height, 2):
            far_rows(k, (row, row + 1) if height > 1 else (row,))

    for k in range(4, -1, -1):
        height = HEIGHTS[k]
        part_high, part_low = halves(loc[:, pl.ds(0, LANES * height)])
        dropped = dot(drop_ref[...], jnp.concatenate([part_high, part_low, part_high], axis=0))
        for row in range(height):
            here = dropped[:, LANES * row : LANES * (row + 1)] + fars[pl.ds(FAMILY * (OFFSETS[k] + row), FAMILY), :]
            paired[pl.ds(40 * row, 40), :] = jnp.concatenate([here[:40], here[40:]], axis=1)
        part_high, part_low = halves(paired[pl.ds(0, 40 * height), :])
        joined = dot(jnp.concatenate([part_high, part_low], axis=1), join_ref[...])
        joined_ref[pl.ds(0, 40 * height), :] = joined
        if k > 0:
            for row in range(2 * height):
                loc[pl.ds(0, CHAN), pl.ds(LANES * row, LANES)] = joined_ref[pl.ds(CHAN * row, CHAN), :]

    scale = 1.0 / (2.0 * math.pi)
    for tile in range(4):
        rows = pl.ds(8 * tile, 8)
        terms = [joined_ref[pl.ds(8 * tile * CHAN + c, 8, stride=CHAN), :] for c in range(CHAN)]

        def value(j, _, terms=terms, rows=rows):
            x, y = own[0, j, rows, :], own[1, j, rows, :]
            re, im = terms[ORDER - 1], terms[CHAN - 1]
            for l in range(ORDER - 2, -1, -1):
                re, im = re * x - im * y + terms[l], re * y + im * x + terms[ORDER + l]
            out[0, j, rows, :] = (im - near[1, j, rows, :]) * scale
            out[1, j, rows, :] = (re + near[0, j, rows, :]) * scale
            return 0

        lax.fori_loop(0, 16, value, 0, unroll=2)


def params():
    return pltpu.CompilerParams(vmem_limit_bytes=VMEM)


def shape(*sizes):
    return jax.ShapeDtypeStruct(sizes, f32)


def neighbours(value, axis, step):
    size = lax.axis_size(axis)
    return lax.ppermute(value, axis, [(i, (i + step) % size) for i in range(size)])


def fields(own, place):
    smem = pl.BlockSpec(memory_space=pltpu.SMEM)
    vmem = pl.BlockSpec(memory_space=pltpu.VMEM)
    other = lax.ppermute(own, "rep", [(0, 1), (1, 0)])
    lift_high, lift_low = halves_np(upward_family())
    lift = np.zeros((32, 3 * FAMILY), jnp.bfloat16)
    lift[:CHAN] = np.concatenate([lift_high, lift_high, lift_low], axis=1)
    cells, packed, coarse = pl.pallas_call(
        upward_kernel,
        out_shape=(shape(ROWS * FAMILY, LANES), shape(2, 32 + FAMILY, LANES), shape(64, LANES)),
        scratch_shapes=[pltpu.VMEM((640, LANES), f32), pltpu.VMEM((320, LANES), f32)],
        compiler_params=params(),
        name="upward",
    )(own, other, jnp.asarray(split_lanes()), jnp.asarray(lift), jnp.asarray(quarter_lanes().T.copy()))
    from_left = neighbours(packed[1], "cell", 1)
    from_right = neighbours(packed[0], "cell", -1)
    gathered = lax.all_to_all(coarse, ("cell", "level"), 0, 0, tiled=True)
    sides = shape(32 + FAMILY, LANES)
    rows, from_left, from_right = pl.pallas_call(
        rows_kernel,
        in_specs=[smem] + [vmem] * 5,
        out_shape=(shape(2, 104 + 2 * FAMILY, LANES), sides, sides),
        compiler_params=params(),
        name="rows",
    )(place, own, other, cells, from_left, from_right)
    above = neighbours(rows[1], "level", 1)
    below = neighbours(rows[0], "level", -1)
    near = pl.pallas_call(
        near_kernel,
        in_specs=[smem] + [vmem] * 6,
        out_shape=shape(2, 16, 32, LANES),
        scratch_shapes=[
            pltpu.VMEM((3, 96, 48, LANES), f32),
            pltpu.VMEM((104, LANES), f32),
            pltpu.VMEM((104, LANES), f32),
        ],
        compiler_params=params(),
        name="near",
    )(place, own, other, from_left, from_right, above, below)
    far_high, far_low = halves_np(far_family())
    drop_table = np.zeros((FAMILY, 32))
    drop_table[:, :CHAN] = downward_family()
    drop_high, drop_low = halves_np(drop_table)
    to_top, near5, from_top, top = coarse_tables()
    tables = [
        np.concatenate([far_high, far_low], axis=0),
        np.concatenate([drop_high, drop_high, drop_low], axis=1),
        join_lanes(),
        np.concatenate([quarter_lanes()] * 2, axis=0).astype(jnp.bfloat16),
        side_by_side(to_top.reshape(4 * LANES, LANES)),
        side_by_side(near5.reshape(4, 12 * LANES, LANES)),
        packed_table(from_top),
        packed_table(top),
    ]
    operands = [own, near, cells, from_left, from_right, above, below, gathered] + [
        jnp.asarray(table) for table in tables
    ]
    specs = [whole(value.shape) for value in operands]
    specs[13] = pl.BlockSpec((1, 12 * LANES, 2 * LANES), lambda i, place: (place[1], 0, 0))
    specs[14] = pl.BlockSpec((1, LANES, LANES), lambda i, place: (place[1], 0, 0))
    return pl.pallas_call(
        far_kernel,
        grid_spec=pltpu.PrefetchScalarGridSpec(
            num_scalar_prefetch=1,
            grid=(1,),
            in_specs=specs,
            out_specs=whole((2, 16, 32, LANES)),
            scratch_shapes=[
                pltpu.VMEM((41 * FAMILY, LANES), bf16),
                pltpu.VMEM((41 * FAMILY, LANES), bf16),
                pltpu.VMEM((ROWS * FAMILY, LANES), f32),
                pltpu.VMEM((640, 2 * LANES), f32),
                pltpu.VMEM((640, LANES), f32),
                pltpu.VMEM((32, 16 * LANES), f32),
            ],
        ),
        out_shape=shape(2, 16, 32, LANES),
        compiler_params=params(),
        name="far",
    )(place, *operands)


def flat_index(shape_):
    rows = lax.broadcasted_iota(jnp.int32, shape_, 0)
    return rows * LANES + lax.broadcasted_iota(jnp.int32, shape_, 1)


def swap_step(arrays, bit, high, descending, lanes):
    distance = 1 << bit

    def partner(value):
        if distance >= LANES:
            step = distance // LANES
            down = pltpu.roll(value, step, 0)
            return down if step == 4 else jnp.where(high, down, pltpu.roll(value, 8 - step, 0))
        if distance == 64:
            return pltpu.roll(value, 64, 1)
        return jnp.take_along_axis(value, lanes ^ distance, axis=1)

    key = arrays[0]
    other = partner(key)
    flip = high if descending is False else (~high if descending is True else high ^ descending)
    take = (other < key) ^ flip
    return [jnp.where(take, other, key)] + [jnp.where(take, partner(x), x) for x in arrays[1:]]


def bitonic(tiles, first_block, last_block):
    index = flat_index((8, LANES))
    lanes = lax.broadcasted_iota(jnp.int32, (8, LANES), 1)
    highs = [(index & (1 << bit)) != 0 for bit in range(10)]
    count = len(tiles)
    for block in range(first_block, last_block + 1):

        def descending(v):
            if block == last_block:
                return False
            return bool((v >> (block - 10)) & 1) if block >= 10 else highs[block]

        for bit in range(block - 1, -1, -1):
            if bit >= 10:
                step = 1 << (bit - 10)
                for v in range(count):
                    if v & step:
                        continue
                    low, high = tiles[v], tiles[v + step]
                    take = high[0] > low[0] if descending(v) else high[0] < low[0]
                    tiles[v] = [jnp.where(take, y, x) for x, y in zip(low, high)]
                    tiles[v + step] = [jnp.where(take, x, y) for x, y in zip(low, high)]
            else:
                for v in range(count):
                    tiles[v] = swap_step(tiles[v], bit, highs[bit], descending(v), lanes)
    return tiles


def pack_kernel(place_ref, pos, strength, owner_ref, leaf, slot, out, keys, values):
    odd = place_ref[0] % 2
    owner = owner_ref[...]
    address = slot[...] * 4096 + leaf[...]
    address = jnp.where(odd == 1, 65535 - address, address)
    key = owner * 65536 + address
    starts = []
    for o in range(16):
        bound = jnp.where(odd == 1, o + 1, o)
        before = (owner < bound).astype(jnp.int32)
        before = before[0:8] + before[8:16] + before[16:24] + before[24:32]
        starts.append(jnp.sum(before) + jnp.where(odd == 1, 0, 1024))
    loads = (key, pos[0], pos[1], strength[...])
    tiles = bitonic([[load[8 * v : 8 * v + 8] for load in loads] for v in range(4)], 1, 12)
    keys[...] = jnp.full(keys.shape, -1, jnp.int32)
    for v in range(4):
        keys[pl.ds(8 + 8 * v, 8), :] = tiles[v][0]
        for c in range(3):
            values[c, pl.ds(8 + 8 * v, 8), :] = tiles[v][1 + c]
    lane = lane_index(8)
    for o in range(16):
        start = starts[o]
        row = start // LANES
        shift = start % LANES
        back = jnp.where(shift == 0, 0, LANES - shift)

        def window(ref):
            upper = pltpu.roll(ref[pl.ds(row, 8), :], back, 1)
            lower = pltpu.roll(ref[pl.ds(row + 1, 8), :], back, 1)
            return jnp.where(lane < LANES - shift, upper, lower)

        mine = window(keys)
        place = mine - o * 65536
        valid = (place >= 0) & (place < 65536)
        place = jnp.where(odd == 1, 65535 - place, place)
        out[o, 3] = jnp.where(valid, place, 65536).astype(f32)
        for c in range(3):
            out[o, c] = window(values.at[c])


def settle_kernel(arrived, pos, strength, out, marks_a, marks_b, loads_a, loads_b):
    tiles = bitonic([[arrived[v, c] for c in (3, 0, 1, 2)] for v in range(16)], 11, 14)
    index = flat_index((8, LANES))
    for ref in (marks_a, marks_b):
        ref[...] = jnp.zeros(ref.shape, jnp.int32)
    for v in range(16):
        address = tiles[v][0].astype(jnp.int32)
        rows = pl.ds(64 + 8 * v, 8)
        marks_a[rows, :] = jnp.where(address < 65536, 2 * (address - index - 1024 * v) + 1, 0)
        for c in range(3):
            loads_a[c, rows, :] = tiles[v][1 + c]
    lane = lane_index(64)
    marks, values = (marks_a, marks_b), (loads_a, loads_b)
    for bit in range(15, -1, -1):
        now, later = marks[bit % 2 == 0], marks[bit % 2]
        load_now, load_later = values[bit % 2 == 0], values[bit % 2]
        test = 2 << bit
        rows = (1 << bit) // LANES
        for base in range(0, 512, 64):
            here = pl.ds(base + 64, 64)
            own = now[here, :]
            own = jnp.where((own & test) != 0, 0, own)
            if rows >= 64 and base < rows:
                later[here, :] = own
                for c in range(3):
                    load_later[c, here, :] = load_now[c, here, :]
                continue

            def source(ref):
                if rows:
                    return ref[pl.ds(base + 64 - rows, 64), :]
                mixed = jnp.where(
                    lane >= LANES - (1 << bit), ref[pl.ds(base + 63, 64), :], ref[here, :]
                )
                return pltpu.roll(mixed, 1 << bit, 1)

            there = source(now)
            come = (there & test) != 0
            later[here, :] = jnp.where(come, there, own)
            for c in range(3):
                load_later[c, here, :] = jnp.where(come, source(load_now.at[c]), load_now[c, here, :])
    for j in range(16):
        rows = pl.ds(64 + 32 * j, 32)
        moved = marks_a[rows, :] != 0
        out[0, j] = jnp.where(moved, loads_a[0, rows, :], pos[0, j])
        out[1, j] = jnp.where(moved, loads_a[1, rows, :], pos[1, j])
        out[2, j] = jnp.where(moved, loads_a[2, rows, :], strength[j])


def local(
    resident_pos, resident_strength, mover_pos, mover_strength, mover_owner, mover_leaf, mover_slot
):
    smem = pl.BlockSpec(memory_space=pltpu.SMEM)
    vmem = pl.BlockSpec(memory_space=pltpu.VMEM)
    place = jnp.stack([lax.axis_index("cell"), lax.axis_index("level")]).astype(jnp.int32)
    outgoing = pl.pallas_call(
        pack_kernel,
        in_specs=[smem] + [vmem] * 5,
        out_shape=shape(16, 4, 8, LANES),
        scratch_shapes=[pltpu.VMEM((56, LANES), jnp.int32), pltpu.VMEM((3, 56, LANES), f32)],
        compiler_params=params(),
        name="pack",
    )(
        place,
        mover_pos.reshape(2, 32, LANES),
        mover_strength.reshape(32, LANES),
        mover_owner.reshape(32, LANES),
        mover_leaf.reshape(32, LANES),
        mover_slot.reshape(32, LANES),
    )
    arrived = lax.all_to_all(outgoing, "cell", 0, 0, tiled=True)
    own = pl.pallas_call(
        settle_kernel,
        out_shape=shape(3, 16, 32, LANES),
        scratch_shapes=[
            pltpu.VMEM((576, LANES), jnp.int32),
            pltpu.VMEM((576, LANES), jnp.int32),
            pltpu.VMEM((3, 576, LANES), f32),
            pltpu.VMEM((3, 576, LANES), f32),
        ],
        compiler_params=params(),
        name="settle",
    )(arrived, resident_pos, resident_strength)
    return fields(own, place)


def solution(mesh):
    return jax.shard_map(
        local,
        mesh=mesh,
        in_specs=(
            P(None, "rep", "level", "cell"),
            P("rep", "level", "cell"),
            P(None, "rep", "level", "cell"),
            P("rep", "level", "cell"),
            P("rep", "level", "cell"),
            P("rep", "level", "cell"),
            P("rep", "level", "cell"),
        ),
        out_specs=P(None, "rep", "level", "cell"),
        check_vma=False,
    )
```

```python
import functools
import math

import jax
import jax.numpy as jnp
import numpy as np
from jax import lax
from jax.experimental import pallas as pl
from jax.experimental.pallas import tpu as pltpu
from jax.sharding import PartitionSpec as P

ORDER = 10
CHAN = 2 * ORDER
FAMILY = 4 * CHAN
CAP = 1024
BLOB = 0.09
LANES = 128
HEIGHTS = (16, 8, 4, 2, 1)
WIDTHS = (64, 32, 16, 8, 4)
OFFSETS = (0, 16, 24, 28, 30)
ROWS = 31
PACKS = (None, 0, 34, 52, 62)
VMEM = 56 * 2**20

f32 = jnp.float32
bf16 = jnp.bfloat16
precise = lax.Precision.HIGHEST


def real_form(matrix):
    top_rows = np.concatenate([matrix.real, -matrix.imag], axis=1)
    low_rows = np.concatenate([matrix.imag, matrix.real], axis=1)
    return np.concatenate([top_rows, low_rows], axis=0)


def child_offset(parity_x, parity_y):
    return complex((parity_x - 0.5) / 2.0, (parity_y - 0.5) / 2.0)


def upward_table(parity_x, parity_y):
    offset = child_offset(parity_x, parity_y)
    matrix = np.zeros((ORDER, ORDER), complex)
    for k in range(ORDER):
        for m in range(k + 1):
            matrix[k, m] = math.comb(k, m) * 0.5**m * offset ** (k - m)
    return real_form(matrix)


def downward_table(parity_x, parity_y):
    offset = child_offset(parity_x, parity_y)
    matrix = np.zeros((ORDER, ORDER), complex)
    for m in range(ORDER):
        for l in range(m, ORDER):
            matrix[m, l] = 0.5 ** (m + 1) * math.comb(l, m) * offset ** (l - m)
    return real_form(matrix)


def far_table(step_x, step_y):
    distance = complex(step_x, step_y)
    matrix = np.zeros((ORDER, ORDER), complex)
    for l in range(ORDER):
        for k in range(ORDER):
            matrix[l, k] = (-1) ** (k + 1) * math.comb(k + l, l) * distance ** (-(k + l + 1))
    return real_form(matrix)


def family(parity_x, parity_y):
    first = (2 * parity_x + parity_y) * CHAN
    return slice(first, first + CHAN)


def upward_family():
    table = np.zeros((CHAN, FAMILY))
    for b in (0, 1):
        for a in (0, 1):
            table[:, family(b, a)] = upward_table(b, a)
    return table


def downward_family():
    table = np.zeros((FAMILY, CHAN))
    for b in (0, 1):
        for a in (0, 1):
            table[family(b, a), :] = downward_table(b, a)
    return table


def far_family():
    table = np.zeros((3, FAMILY, 3, FAMILY))
    for dx in (-1, 0, 1):
        for dy in (-1, 0, 1):
            for bt in (0, 1):
                for at in (0, 1):
                    for bs in (0, 1):
                        for as_ in (0, 1):
                            step_x = 2 * dx + bs - bt
                            step_y = 2 * dy + as_ - at
                            if max(abs(step_x), abs(step_y)) >= 2:
                                table[dx + 1, family(bt, at), dy + 1, family(bs, as_)] = far_table(
                                    step_x, step_y
                                )
    return table.reshape(3 * FAMILY, 3 * FAMILY)


def coarse_tables():
    far5 = {}
    to_top = np.zeros((4, LANES, LANES))
    near5 = np.zeros((4, 12, LANES, LANES))
    from_top = np.zeros((4, LANES, LANES))
    lane = lambda column: np.arange(CHAN) * 4 + column
    for row in range(4):
        for column in range(4):
            lift = upward_table(column // 2, row // 2) @ upward_table(column % 2, row % 2)
            to_top[row][np.ix_(lane(column), np.arange(CHAN))] = lift.T
            drop = downward_table(column % 2, row % 2) @ downward_table(column // 2, row // 2)
            from_top[row][np.ix_(np.arange(CHAN), lane(column))] = drop.T
    for row in range(4):
        for column in range(4):
            down = downward_table(column % 2, row % 2)
            x = 4 + column
            for step in range(3):
                for other_row in range(4):
                    for other in range(4):
                        u = 4 * step + other
                        total = np.zeros((CHAN, CHAN))
                        if abs(u // 2 - x // 2) <= 1:
                            if max(abs(u - x), abs(other_row - row)) >= 2:
                                total += far_table(u - x, other_row - row)
                        if abs(u // 2 - x // 2) >= 2:
                            key = (u // 2 - x // 2, other_row // 2 - row // 2)
                            if key not in far5:
                                far5[key] = far_table(*key)
                            total += down @ far5[key] @ upward_table(other % 2, other_row % 2)
                        near5[row, step * 4 + other_row][np.ix_(lane(other), lane(column))] += total.T
    top = np.zeros((LANES, 32 * 32))
    for step in range(-15, 16):
        if abs(step) >= 2:
            top[:CHAN, (step + 15) * 32 : (step + 15) * 32 + CHAN] = far_table(step, 0).T
    return to_top, near5, from_top, top


def halves_np(table):
    high = np.asarray(table, np.float32).astype(jnp.bfloat16)
    low = (np.asarray(table, np.float32) - high.astype(np.float32)).astype(jnp.bfloat16)
    return high, low


def split_lanes():
    table = np.zeros((LANES, LANES), np.float32)
    x = np.arange(LANES)
    table[x, 64 * (x % 2) + x // 2] = 1.0
    return np.concatenate([table, table], axis=0).astype(jnp.bfloat16)


def join_lanes():
    table = np.zeros((2, LANES, LANES), np.float32)
    x = np.arange(64)
    table[0, x, 2 * x] = 1.0
    table[1, x, 2 * x + 1] = 1.0
    table = table.reshape(2 * LANES, LANES)
    return np.concatenate([table, table], axis=0).astype(jnp.bfloat16)


def quarter_lanes():
    k = np.arange(LANES)
    return (k[:, None] % 4 == k[None, :]).astype(np.float32)


def halves(value):
    high = value.astype(bf16)
    return high, (value - high.astype(f32)).astype(bf16)


def dot(left, right):
    return jnp.dot(left, right, preferred_element_type=f32)


def lane_index(rows):
    return lax.broadcasted_iota(jnp.int32, (rows, LANES), 1)


def whole(shape):
    return pl.BlockSpec(shape, lambda *_: (0,) * len(shape))


def upward_kernel(
    after, own, other, split_ref, lift_ref, spread_ref, cells, to_left, to_right, top, bottom, coarse, mom, raw
):
    for tile in range(4):
        rows = pl.ds(8 * tile, 8)

        def add_slot(j, sums):
            for ref in (own, other):
                x, y, re = ref[0, j, rows, :], ref[1, j, rows, :], ref[2, j, rows, :]
                real, imag = list(sums[:ORDER]), list(sums[ORDER:])
                real[0] = real[0] + re
                im = re * y
                re = re * x
                real[1] = real[1] + re
                imag[1] = imag[1] + im
                for k in range(2, ORDER):
                    re, im = re * x - im * y, re * y + im * x
                    real[k] = real[k] + re
                    imag[k] = imag[k] + im
                sums = tuple(real + imag)
            return sums

        sums = lax.fori_loop(
            0, 16, add_slot, tuple(jnp.zeros((8, LANES), f32) for _ in range(CHAN)), unroll=2
        )
        for c in range(CHAN):
            mom[pl.ds(8 * tile * CHAN + c, 8, stride=CHAN), :] = sums[c]

    lane40 = lane_index(40)
    lane80 = lane_index(FAMILY)
    first = jnp.zeros((FAMILY, LANES), f32)
    last = jnp.zeros((FAMILY, LANES), f32)
    ends = [jnp.zeros((FAMILY, LANES), f32)] * 2
    for k, height in enumerate(HEIGHTS):
        source = mom[...] if k == 0 else raw[pl.ds(0, 40 * height), :]
        spread = dot(jnp.concatenate(halves(source), axis=1), split_ref[...])
        parents = []
        for row in range(height):
            block = spread[40 * row : 40 * row + 40]
            even = jnp.where(lane40 < 64, block, 0.0)
            odd = jnp.where(lane40 < 64, pltpu.roll(block, 64, 1), 0.0)
            parent = jnp.concatenate([even, odd], axis=0)
            index = OFFSETS[k] + row
            cells[pl.ds(FAMILY * index, FAMILY), :] = parent
            first = jnp.where(lane80 == index, pltpu.roll(parent, index, 1), first)
            last = jnp.where(
                lane80 == index, pltpu.roll(parent, (index - WIDTHS[k] + 1) % LANES, 1), last
            )
            parents.append(parent)
            for side, ref in enumerate((top, bottom)):
                if row != (height - 1) * side:
                    continue
                if k == 0:
                    ref[pl.ds(104, FAMILY), :] = parent
                else:
                    inside = (lane80 > PACKS[k]) & (lane80 <= PACKS[k] + WIDTHS[k])
                    ends[side] = jnp.where(inside, pltpu.roll(parent, PACKS[k] + 1, 1), ends[side])
        high, low = halves(jnp.concatenate(parents, axis=1))
        lifted = dot(lift_ref[...], jnp.concatenate([high, low, high], axis=0))
        for row in range(height):
            raw[pl.ds(CHAN * row, CHAN), :] = lifted[:CHAN, LANES * row : LANES * (row + 1)]
    to_left[pl.ds(32, FAMILY), :] = first
    to_right[pl.ds(32, FAMILY), :] = last
    for side, ref in enumerate((top, bottom)):
        ref[pl.ds(104 + FAMILY, FAMILY), :] = ends[side]
        ref[pl.ds(96, 8), :] = jnp.zeros((8, LANES), f32)
        for half, source in enumerate((own, other)):
            for comp in range(3):
                for j in range(16):
                    ref[pl.ds(comp * 32 + half * 16 + j, 1), :] = source[comp, j, pl.ds(31 * side, 1), :]

    four = jnp.dot(raw[pl.ds(0, 24), :], spread_ref[...], precision=precise)
    row24 = lax.broadcasted_iota(jnp.int32, (24, LANES), 0)
    line = jnp.sum(jnp.where((lane_index(24) // 4 == row24) & (row24 < CHAN), four, 0.0), axis=0, keepdims=True)
    coarse[...] = jnp.broadcast_to(line, coarse.shape)

    lane32 = lane_index(32)

    left = right = jnp.zeros((32, LANES), f32)
    for half, ref in enumerate((own, other)):
        for comp in range(3):
            for j in range(16):
                m = comp * 32 + half * 16 + j
                value = ref[comp, j]
                left = jnp.where(lane32 == m, pltpu.roll(value, m, 1), left)
                right = jnp.where(lane32 == m, pltpu.roll(value, m + 1, 1), right)
    to_left[pl.ds(0, 32), :] = left
    to_right[pl.ds(0, 32), :] = right


def ring_columns(parent, k, index, from_left, from_right, lane):
    width = WIDTHS[k]
    parent = jnp.where(lane == LANES - 1, pltpu.roll(from_left, (LANES - 1 - index) % LANES, 1), parent)
    return jnp.where(lane == width, pltpu.roll(from_right, (width - index) % LANES, 1), parent)


def rows_kernel(place, after, top, bottom, came_left, came_right, out_top, out_bottom, from_left, from_right):
    lane80 = lane_index(FAMILY)
    from_left[...] = jnp.where(place[0] > 0, came_left[...], 0.0)
    from_right[...] = jnp.where(place[0] < 15, came_right[...], 0.0)
    left, right = from_left[pl.ds(32, FAMILY), :], from_right[pl.ds(32, FAMILY), :]
    for side, (ref, out) in enumerate(((top, out_top), (bottom, out_bottom))):
        out[pl.ds(0, 104), :] = ref[pl.ds(0, 104), :]
        out[pl.ds(96, 1), :] = from_left[pl.ds(31 * side, 1), :]
        out[pl.ds(97, 1), :] = from_right[pl.ds(31 * side, 1), :]
        out[pl.ds(104, FAMILY), :] = ring_columns(
            ref[pl.ds(104, FAMILY), :], 0, 15 * side, left, right, lane80
        )
        packed = ref[pl.ds(104 + FAMILY, FAMILY), :]
        for k in range(1, 5):
            index = OFFSETS[k] + (HEIGHTS[k] - 1) * side
            start = PACKS[k]
            stop = start + WIDTHS[k] + 1
            packed = jnp.where(lane80 == start, pltpu.roll(left, (start - index) % LANES, 1), packed)
            packed = jnp.where(lane80 == stop, pltpu.roll(right, (stop - index) % LANES, 1), packed)
        out[pl.ds(104 + FAMILY, FAMILY), :] = packed


GROUP = 8


def inside_domain(tile, dy):
    return dy == 0 or (dy == -1 and tile > 0) or (dy == 1 and tile < 3)


def add_sources(acc, own, tile, group, sources, count, unroll):
    rows = pl.ds(8 * tile, 8)
    tx = [own[0, group * GROUP + i, rows, :] for i in range(GROUP)]
    ty = [own[1, group * GROUP + i, rows, :] for i in range(GROUP)]

    def pairs(j, acc):
        acc = list(acc)
        for source in sources:
            sx, sy, q = source(j)
            for i in range(GROUP):
                gap_x = tx[i] - sx
                gap_y = ty[i] - sy
                weight = q * (1.0 / (gap_x * gap_x + (gap_y * gap_y + BLOB)))
                acc[i] = acc[i] + weight * gap_x
                acc[GROUP + i] = acc[GROUP + i] + weight * gap_y
        return tuple(acc)

    return lax.fori_loop(0, count, pairs, acc, unroll=unroll)


def store_group(out, acc, tile, group):
    for i in range(GROUP):
        out[0, group * GROUP + i, pl.ds(8 * tile, 8), :] = acc[i]
        out[1, group * GROUP + i, pl.ds(8 * tile, 8), :] = acc[GROUP + i]


def inner_kernel(own, sources, earlier, after, out, *, add):
    for tile in range(4):
        for group in range(16 // GROUP):
            if add:
                acc = tuple(
                    earlier[part, group * GROUP + i, pl.ds(8 * tile, 8), :]
                    for part in range(2)
                    for i in range(GROUP)
                )
            else:
                acc = tuple(jnp.zeros((8, LANES), f32) for _ in range(2 * GROUP))
            steps = []
            for dy in (-1, 0, 1):
                if not inside_domain(tile, dy):
                    continue

                def source(j, rows=pl.ds(8 * tile + dy, 8), dy=dy):
                    y = sources[1, j, rows, :]
                    return sources[0, j, rows, :], y + float(dy) if dy else y, sources[2, j, rows, :]

                steps.append(source)
            acc = add_sources(acc, own, tile, group, steps, 16, 4)
            store_group(out, acc, tile, group)


def near_kernel(
    place, own, other, inner, from_left, from_right, came_above, came_below, out, src, above, below
):
    above[...] = jnp.where(place[1] > 0, came_above[pl.ds(0, 104), :], 0.0)
    below[...] = jnp.where(place[1] < 3, came_below[pl.ds(0, 104), :], 0.0)
    lane32 = lane_index(32)
    lane1 = lane_index(1)

    for comp in range(3):
        for half, ref in enumerate((own, other)):
            for j in range(16):
                m = comp * 32 + half * 16 + j
                rows = (ref[comp, j], above[pl.ds(m, 1), :], below[pl.ds(m, 1), :])
                lefts = (from_left[pl.ds(0, 32), :], above[pl.ds(96, 1), :], below[pl.ds(96, 1), :])
                rights = (from_right[pl.ds(0, 32), :], above[pl.ds(97, 1), :], below[pl.ds(97, 1), :])
                for part in range(3):
                    place = (pl.ds(8, 32), pl.ds(7, 1), pl.ds(40, 1))[part]
                    lane = lane32 if part == 0 else lane1
                    middle = rows[part]
                    before = pltpu.roll(middle, 1, 1)
                    after = pltpu.roll(middle, LANES - 1, 1)
                    left = pltpu.roll(lefts[part], (LANES - m) % LANES, 1)
                    right = pltpu.roll(rights[part], (LANES - 1 - m) % LANES, 1)
                    before = jnp.where(lane == 0, left, before)
                    after = jnp.where(lane == LANES - 1, right, after)
                    if comp == 0:
                        before = before - 1.0
                        after = after + 1.0
                    src[0, m, place, :] = before
                    src[1, m, place, :] = middle
                    src[2, m, place, :] = after

    for tile in range(4):
        for group in range(16 // GROUP):
            acc = tuple(
                inner[part, group * GROUP + i, pl.ds(8 * tile, 8), :]
                for part in range(2)
                for i in range(GROUP)
            )
            steps = []
            for dy in (-1, 0, 1):
                for dx in range(3):
                    if dx == 1 and inside_domain(tile, dy):
                        continue

                    def source(j, dx=dx, rows=pl.ds(8 + 8 * tile + dy, 8), dy=dy):
                        y = src[dx, 32 + j, rows, :]
                        return src[dx, j, rows, :], y + float(dy) if dy else y, src[dx, 64 + j, rows, :]

                    steps.append(source)
            acc = add_sources(acc, own, tile, group, steps, 32, 2)
            store_group(out, acc, tile, group)


def three_products(value, table):
    product = dot(jnp.concatenate(halves(value), axis=0), table)
    return product[:16, :LANES] + product[16:, :LANES] + product[:16, LANES:]


def packed_parts(value):
    high = value.astype(bf16).astype(f32)
    low = value - high
    return (high + pltpu.roll(low, 32, 1) + pltpu.roll(high, 64, 1)).astype(bf16)


def side_by_side(table):
    return np.concatenate(halves_np(table), axis=-1)


def packed_table(table):
    high, low = halves_np(table)
    out = np.zeros(table.shape, jnp.bfloat16)
    out[..., 0:32, :] = high[..., 0:32, :]
    out[..., 32:64, :] = high[..., 0:32, :]
    out[..., 64:96, :] = low[..., 0:32, :]
    return out


def far_kernel(
    place, own, near, cells, from_left, from_right, above, below, gathered,
    far_ref, drop_ref, join_ref, spread_ref, to_top, near5, from_top, top_ref,
    out, high, low, fars, paired, joined_ref, loc,
):
    cell = place[0]
    level = place[1]
    tops = three_products(
        jnp.concatenate([gathered[pl.ds(row, 16, stride=4), :] for row in range(4)], axis=1), to_top[...]
    )
    spread = dot(packed_parts(tops), top_ref[...])
    source = lax.broadcasted_iota(jnp.int32, (16, 1024), 0)
    step = lax.broadcasted_iota(jnp.int32, (16, 1024), 1) // 32
    line = jnp.sum(jnp.where(step == source - cell + 15, spread, 0.0), axis=0, keepdims=True)
    total = line[:, :LANES]
    for block in range(1, 8):
        total = total + line[:, LANES * block : LANES * (block + 1)]
    total = jnp.broadcast_to(total, (16, LANES))
    total = total + pltpu.roll(total, 64, 1)
    total = total + pltpu.roll(total, 32, 1)
    total = jnp.where(lane_index(16) < CHAN, total, 0.0)
    around = []
    for step in range(3):
        there = cell + step - 1
        inside = (there >= 0) & (there < 16)
        there = jnp.clip(there, 0, 15)
        for row in range(4):
            value = gathered[pl.ds(there * 4 + row, 1), :]
            around.append(jnp.broadcast_to(jnp.where(inside, value, 0.0), (16, LANES)))
    five = dot(packed_parts(total), from_top[0]) + three_products(
        jnp.concatenate(around, axis=1), near5[0]
    )
    five = jnp.broadcast_to(five[0:1], (32, LANES))
    row32 = lax.broadcasted_iota(jnp.int32, (32, LANES), 0)
    five = jnp.where((lane_index(32) // 4 == row32) & (row32 < CHAN), five, 0.0)
    loc[...] = jnp.zeros(loc.shape, f32)
    loc[pl.ds(0, 32), pl.ds(0, LANES)] = dot(
        jnp.concatenate(halves(five), axis=1), spread_ref[...]
    )

    lane80 = lane_index(FAMILY)
    left, right = from_left[pl.ds(32, FAMILY), :], from_right[pl.ds(32, FAMILY), :]
    start = 0
    starts = []
    for k, height in enumerate(HEIGHTS):
        starts.append(start)
        for row in range(-1, height + 1):
            if row in (-1, height):
                ref = above if row == -1 else below
                inside = level > 0 if row == -1 else level < 3
                if k == 0:
                    parent = ref[pl.ds(104, FAMILY), :]
                else:
                    packed = ref[pl.ds(104 + FAMILY, FAMILY), :]
                    parent = pltpu.roll(packed, LANES - PACKS[k] - 1, 1)
                    parent = jnp.where((lane80 <= WIDTHS[k]) | (lane80 == LANES - 1), parent, 0.0)
            else:
                index = OFFSETS[k] + row
                parent = cells[pl.ds(FAMILY * index, FAMILY), :]
                parent = ring_columns(parent, k, index, left, right, lane80)
            if row in (-1, height):
                parent = jnp.where(inside, parent, 0.0)
            part_high, part_low = halves(parent)
            high[pl.ds(FAMILY * start, FAMILY), :] = part_high
            low[pl.ds(FAMILY * start, FAMILY), :] = part_low
            start += 1

    def far_rows(k, rows):
        both = []
        for ref in (high, low):
            both.append(
                jnp.concatenate(
                    [ref[pl.ds(FAMILY * (starts[k] + row), 3 * FAMILY), :] for row in rows], axis=1
                )
            )
        size = 3 * FAMILY
        product = dot(far_ref[...], both[0])
        product = product[:size] + product[size:] + dot(far_ref[pl.ds(0, size), :], both[1])
        for place_, row in enumerate(rows):
            part = product[:, LANES * place_ : LANES * (place_ + 1)]
            fars[pl.ds(FAMILY * (OFFSETS[k] + row), FAMILY), :] = (
                part[FAMILY : 2 * FAMILY]
                + pltpu.roll(part[:FAMILY], 1, 1)
                + pltpu.roll(part[2 * FAMILY :], LANES - 1, 1)
            )

    for k, height in enumerate(HEIGHTS):
        for row in range(0, height, 2):
            far_rows(k, (row, row + 1) if height > 1 else (row,))

    for k in range(4, -1, -1):
        height = HEIGHTS[k]
        part_high, part_low = halves(loc[:, pl.ds(0, LANES * height)])
        dropped = dot(drop_ref[...], jnp.concatenate([part_high, part_low, part_high], axis=0))
        for row in range(height):
            here = dropped[:, LANES * row : LANES * (row + 1)] + fars[pl.ds(FAMILY * (OFFSETS[k] + row), FAMILY), :]
            paired[pl.ds(40 * row, 40), :] = jnp.concatenate([here[:40], here[40:]], axis=1)
        part_high, part_low = halves(paired[pl.ds(0, 40 * height), :])
        joined = dot(jnp.concatenate([part_high, part_low], axis=1), join_ref[...])
        joined_ref[pl.ds(0, 40 * height), :] = joined
        if k > 0:
            for row in range(2 * height):
                loc[pl.ds(0, CHAN), pl.ds(LANES * row, LANES)] = joined_ref[pl.ds(CHAN * row, CHAN), :]

    scale = 1.0 / (2.0 * math.pi)
    for tile in range(4):
        rows = pl.ds(8 * tile, 8)
        terms = [joined_ref[pl.ds(8 * tile * CHAN + c, 8, stride=CHAN), :] for c in range(CHAN)]

        def value(j, _, terms=terms, rows=rows):
            x, y = own[0, j, rows, :], own[1, j, rows, :]
            re, im = terms[ORDER - 1], terms[CHAN - 1]
            for l in range(ORDER - 2, -1, -1):
                re, im = re * x - im * y + terms[l], re * y + im * x + terms[ORDER + l]
            out[0, j, rows, :] = (im - near[1, j, rows, :]) * scale
            out[1, j, rows, :] = (re + near[0, j, rows, :]) * scale
            return 0

        lax.fori_loop(0, 16, value, 0, unroll=2)


def params():
    return pltpu.CompilerParams(vmem_limit_bytes=VMEM)


def shape(*sizes):
    return jax.ShapeDtypeStruct(sizes, f32)


def neighbours(value, axis, step):
    size = lax.axis_size(axis)
    return lax.ppermute(value, axis, [(i, (i + step) % size) for i in range(size)])


def fields(own, place):
    smem = pl.BlockSpec(memory_space=pltpu.SMEM)
    vmem = pl.BlockSpec(memory_space=pltpu.VMEM)
    anywhere = pl.BlockSpec(memory_space=pl.ANY)
    other = lax.ppermute(own, "rep", [(0, 1), (1, 0)])
    inner = pl.pallas_call(
        lambda own, out: inner_kernel(own, own, None, None, out, add=False),
        out_shape=shape(2, 16, 32, LANES),
        compiler_params=params(),
        name="inner_own",
    )(own)
    lift_high, lift_low = halves_np(upward_family())
    lift = np.zeros((32, 3 * FAMILY), jnp.bfloat16)
    lift[:CHAN] = np.concatenate([lift_high, lift_high, lift_low], axis=1)
    message = shape(104 + 2 * FAMILY, LANES)
    sides = shape(32 + FAMILY, LANES)
    cells, to_left, to_right, top, bottom, coarse = pl.pallas_call(
        upward_kernel,
        in_specs=[anywhere] + [vmem] * 5,
        out_shape=(shape(ROWS * FAMILY, LANES), sides, sides, message, message, shape(64, LANES)),
        scratch_shapes=[pltpu.VMEM((640, LANES), f32), pltpu.VMEM((320, LANES), f32)],
        compiler_params=params(),
        name="upward",
    )(inner, own, other, jnp.asarray(split_lanes()), jnp.asarray(lift), jnp.asarray(quarter_lanes().T.copy()))
    from_left = neighbours(to_right, "cell", 1)
    from_right = neighbours(to_left, "cell", -1)
    gathered = lax.all_to_all(coarse, ("cell", "level"), 0, 0, tiled=True)
    inner = pl.pallas_call(
        functools.partial(inner_kernel, add=True),
        in_specs=[vmem] * 3 + [anywhere],
        out_shape=shape(2, 16, 32, LANES),
        compiler_params=params(),
        name="inner",
    )(own, other, inner, cells)
    top, bottom, from_left, from_right = pl.pallas_call(
        rows_kernel,
        in_specs=[smem, anywhere] + [vmem] * 4,
        out_shape=(message, message, sides, sides),
        compiler_params=params(),
        name="rows",
    )(place, inner, top, bottom, from_left, from_right)
    above = neighbours(bottom, "level", 1)
    below = neighbours(top, "level", -1)
    near = pl.pallas_call(
        near_kernel,
        in_specs=[smem] + [vmem] * 7,
        out_shape=shape(2, 16, 32, LANES),
        scratch_shapes=[
            pltpu.VMEM((3, 96, 48, LANES), f32),
            pltpu.VMEM((104, LANES), f32),
            pltpu.VMEM((104, LANES), f32),
        ],
        compiler_params=params(),
        name="near",
    )(place, own, other, inner, from_left, from_right, above, below)
    far_high, far_low = halves_np(far_family())
    drop_table = np.zeros((FAMILY, 32))
    drop_table[:, :CHAN] = downward_family()
    drop_high, drop_low = halves_np(drop_table)
    to_top, near5, from_top, top = coarse_tables()
    tables = [
        np.concatenate([far_high, far_low], axis=0),
        np.concatenate([drop_high, drop_high, drop_low], axis=1),
        join_lanes(),
        np.concatenate([quarter_lanes()] * 2, axis=0).astype(jnp.bfloat16),
        side_by_side(to_top.reshape(4 * LANES, LANES)),
        side_by_side(near5.reshape(4, 12 * LANES, LANES)),
        packed_table(from_top),
        packed_table(top),
    ]
    operands = [own, near, cells, from_left, from_right, above, below, gathered] + [
        jnp.asarray(table) for table in tables
    ]
    specs = [whole(value.shape) for value in operands]
    specs[13] = pl.BlockSpec((1, 12 * LANES, 2 * LANES), lambda i, place: (place[1], 0, 0))
    specs[14] = pl.BlockSpec((1, LANES, LANES), lambda i, place: (place[1], 0, 0))
    return pl.pallas_call(
        far_kernel,
        grid_spec=pltpu.PrefetchScalarGridSpec(
            num_scalar_prefetch=1,
            grid=(1,),
            in_specs=specs,
            out_specs=whole((2, 16, 32, LANES)),
            scratch_shapes=[
                pltpu.VMEM((41 * FAMILY, LANES), bf16),
                pltpu.VMEM((41 * FAMILY, LANES), bf16),
                pltpu.VMEM((ROWS * FAMILY, LANES), f32),
                pltpu.VMEM((640, 2 * LANES), f32),
                pltpu.VMEM((640, LANES), f32),
                pltpu.VMEM((32, 16 * LANES), f32),
            ],
        ),
        out_shape=shape(2, 16, 32, LANES),
        compiler_params=params(),
        name="far",
    )(place, *operands)


def flat_index(shape_):
    rows = lax.broadcasted_iota(jnp.int32, shape_, 0)
    return rows * LANES + lax.broadcasted_iota(jnp.int32, shape_, 1)


def swap_step(arrays, bit, high, descending, lanes):
    distance = 1 << bit

    def partner(value):
        if distance >= LANES:
            step = distance // LANES
            down = pltpu.roll(value, step, 0)
            return down if step == 4 else jnp.where(high, down, pltpu.roll(value, 8 - step, 0))
        if distance == 64:
            return pltpu.roll(value, 64, 1)
        return jnp.take_along_axis(value, lanes ^ distance, axis=1)

    key = arrays[0]
    other = partner(key)
    flip = high if descending is False else (~high if descending is True else high ^ descending)
    take = (other < key) ^ flip
    return [jnp.where(take, other, key)] + [jnp.where(take, partner(x), x) for x in arrays[1:]]


def bitonic(tiles, first_block, last_block):
    index = flat_index((8, LANES))
    lanes = lax.broadcasted_iota(jnp.int32, (8, LANES), 1)
    highs = [(index & (1 << bit)) != 0 for bit in range(10)]
    count = len(tiles)
    for block in range(first_block, last_block + 1):

        def descending(v):
            if block == last_block:
                return False
            return bool((v >> (block - 10)) & 1) if block >= 10 else highs[block]

        for bit in range(block - 1, -1, -1):
            if bit >= 10:
                step = 1 << (bit - 10)
                for v in range(count):
                    if v & step:
                        continue
                    low, high = tiles[v], tiles[v + step]
                    take = high[0] > low[0] if descending(v) else high[0] < low[0]
                    tiles[v] = [jnp.where(take, y, x) for x, y in zip(low, high)]
                    tiles[v + step] = [jnp.where(take, x, y) for x, y in zip(low, high)]
            else:
                for v in range(count):
                    tiles[v] = swap_step(tiles[v], bit, highs[bit], descending(v), lanes)
    return tiles


def pack_kernel(pos, strength, owner_ref, leaf, slot, out, keys, values):
    owner = owner_ref[...]
    address = slot[...] * 4096 + leaf[...]
    key = owner * 65536 + address
    starts = []
    for o in range(16):
        before = (owner < o).astype(jnp.int32)
        before = before[0:8] + before[8:16] + before[16:24] + before[24:32]
        starts.append(jnp.sum(before))
    loads = (key, pos[0], pos[1], strength[...])
    tiles = bitonic([[load[8 * v : 8 * v + 8] for load in loads] for v in range(4)], 1, 12)
    keys[...] = jnp.full(keys.shape, -1, jnp.int32)
    for v in range(4):
        keys[pl.ds(8 * v, 8), :] = tiles[v][0]
        for c in range(3):
            values[c, pl.ds(8 * v, 8), :] = tiles[v][1 + c]
    lane = lane_index(8)
    for o in range(16):
        start = starts[o]
        row = start // LANES
        shift = start % LANES
        back = jnp.where(shift == 0, 0, LANES - shift)

        def window(ref):
            mixed = jnp.where(lane < shift, ref[pl.ds(row + 1, 8), :], ref[pl.ds(row, 8), :])
            return pltpu.roll(mixed, back, 1)

        mine = window(keys)
        place = mine - o * 65536
        valid = (place >= 0) & (place < 65536)
        out[o, 3] = jnp.where(valid, place, 65536).astype(f32)
        for c in range(3):
            out[o, c] = window(values.at[c])


def settle_kernel(arrived, pos, strength, out, marks_a, marks_b, loads_a, loads_b):
    tiles = [[arrived[v, c] for c in (3, 0, 1, 2)] for v in range(16)]
    turned = [lax.broadcasted_iota(jnp.int32, (8, LANES), axis) for axis in (0, 1)]
    for v in range(1, 16, 2):
        for c in range(4):
            value = jnp.take_along_axis(tiles[v][c], 7 - turned[0], axis=0)
            tiles[v][c] = jnp.take_along_axis(value, LANES - 1 - turned[1], axis=1)
    tiles = bitonic(tiles, 11, 14)
    index = flat_index((8, LANES))
    for ref in (marks_a, marks_b):
        ref[...] = jnp.zeros(ref.shape, jnp.int32)
    for v in range(16):
        address = tiles[v][0].astype(jnp.int32)
        rows = pl.ds(64 + 8 * v, 8)
        marks_a[rows, :] = jnp.where(address < 65536, 2 * (address - index - 1024 * v) + 1, 0)
        for c in range(3):
            loads_a[c, rows, :] = tiles[v][1 + c]
    lane = lane_index(64)
    marks, values = (marks_a, marks_b), (loads_a, loads_b)
    for bit in range(15, -1, -1):
        now, later = marks[bit % 2 == 0], marks[bit % 2]
        load_now, load_later = values[bit % 2 == 0], values[bit % 2]
        test = 2 << bit
        rows = (1 << bit) // LANES
        for base in range(0, 512, 64):
            here = pl.ds(base + 64, 64)
            own = now[here, :]
            own = jnp.where((own & test) != 0, 0, own)
            if rows >= 64 and base < rows:
                later[here, :] = own
                for c in range(3):
                    load_later[c, here, :] = load_now[c, here, :]
                continue

            def source(ref):
                if rows:
                    return ref[pl.ds(base + 64 - rows, 64), :]
                mixed = jnp.where(
                    lane >= LANES - (1 << bit), ref[pl.ds(base + 63, 64), :], ref[here, :]
                )
                return pltpu.roll(mixed, 1 << bit, 1)

            there = source(now)
            come = (there & test) != 0
            later[here, :] = jnp.where(come, there, own)
            for c in range(3):
                load_later[c, here, :] = jnp.where(come, source(load_now.at[c]), load_now[c, here, :])
    for j in range(16):
        rows = pl.ds(64 + 32 * j, 32)
        moved = marks_a[rows, :] != 0
        out[0, j] = jnp.where(moved, loads_a[0, rows, :], pos[0, j])
        out[1, j] = jnp.where(moved, loads_a[1, rows, :], pos[1, j])
        out[2, j] = jnp.where(moved, loads_a[2, rows, :], strength[j])


def local(
    resident_pos, resident_strength, mover_pos, mover_strength, mover_owner, mover_leaf, mover_slot
):
    place = jnp.stack([lax.axis_index("cell"), lax.axis_index("level")]).astype(jnp.int32)
    outgoing = pl.pallas_call(
        pack_kernel,
        out_shape=shape(16, 4, 8, LANES),
        scratch_shapes=[pltpu.VMEM((56, LANES), jnp.int32), pltpu.VMEM((3, 56, LANES), f32)],
        compiler_params=params(),
        name="pack",
    )(
        mover_pos.reshape(2, 32, LANES),
        mover_strength.reshape(32, LANES),
        mover_owner.reshape(32, LANES),
        mover_leaf.reshape(32, LANES),
        mover_slot.reshape(32, LANES),
    )
    arrived = lax.all_to_all(outgoing, "cell", 0, 0, tiled=True)
    own = pl.pallas_call(
        settle_kernel,
        out_shape=shape(3, 16, 32, LANES),
        scratch_shapes=[
            pltpu.VMEM((576, LANES), jnp.int32),
            pltpu.VMEM((576, LANES), jnp.int32),
            pltpu.VMEM((3, 576, LANES), f32),
            pltpu.VMEM((3, 576, LANES), f32),
        ],
        compiler_params=params(),
        name="settle",
    )(arrived, resident_pos, resident_strength)
    return fields(own, place)


def solution(mesh):
    return jax.shard_map(
        local,
        mesh=mesh,
        in_specs=(
            P(None, "rep", "level", "cell"),
            P("rep", "level", "cell"),
            P(None, "rep", "level", "cell"),
            P("rep", "level", "cell"),
            P("rep", "level", "cell"),
            P("rep", "level", "cell"),
            P("rep", "level", "cell"),
        ),
        out_specs=P(None, "rep", "level", "cell"),
        check_vma=False,
    )
```

```python
import functools
import math

import jax
import jax.numpy as jnp
import numpy as np
from jax import lax
from jax.experimental import pallas as pl
from jax.experimental.pallas import tpu as pltpu
from jax.sharding import PartitionSpec as P

ORDER = 10
CHAN = 2 * ORDER
FAMILY = 4 * CHAN
CAP = 1024
BLOB = 0.09
LANES = 128
HEIGHTS = (16, 8, 4, 2, 1)
WIDTHS = (64, 32, 16, 8, 4)
OFFSETS = (0, 16, 24, 28, 30)
ROWS = 31
PACKS = (None, 0, 34, 52, 62)
VMEM = 56 * 2**20

f32 = jnp.float32
bf16 = jnp.bfloat16
precise = lax.Precision.HIGHEST


def real_form(matrix):
    top_rows = np.concatenate([matrix.real, -matrix.imag], axis=1)
    low_rows = np.concatenate([matrix.imag, matrix.real], axis=1)
    return np.concatenate([top_rows, low_rows], axis=0)


def child_offset(parity_x, parity_y):
    return complex((parity_x - 0.5) / 2.0, (parity_y - 0.5) / 2.0)


def upward_table(parity_x, parity_y):
    offset = child_offset(parity_x, parity_y)
    matrix = np.zeros((ORDER, ORDER), complex)
    for k in range(ORDER):
        for m in range(k + 1):
            matrix[k, m] = math.comb(k, m) * 0.5**m * offset ** (k - m)
    return real_form(matrix)


def downward_table(parity_x, parity_y):
    offset = child_offset(parity_x, parity_y)
    matrix = np.zeros((ORDER, ORDER), complex)
    for m in range(ORDER):
        for l in range(m, ORDER):
            matrix[m, l] = 0.5 ** (m + 1) * math.comb(l, m) * offset ** (l - m)
    return real_form(matrix)


def far_table(step_x, step_y):
    distance = complex(step_x, step_y)
    matrix = np.zeros((ORDER, ORDER), complex)
    for l in range(ORDER):
        for k in range(ORDER):
            matrix[l, k] = (-1) ** (k + 1) * math.comb(k + l, l) * distance ** (-(k + l + 1))
    return real_form(matrix)


def family(parity_x, parity_y):
    first = (2 * parity_x + parity_y) * CHAN
    return slice(first, first + CHAN)


def upward_family():
    table = np.zeros((CHAN, FAMILY))
    for b in (0, 1):
        for a in (0, 1):
            table[:, family(b, a)] = upward_table(b, a)
    return table


def downward_family():
    table = np.zeros((FAMILY, CHAN))
    for b in (0, 1):
        for a in (0, 1):
            table[family(b, a), :] = downward_table(b, a)
    return table


def far_family():
    table = np.zeros((3, FAMILY, 3, FAMILY))
    for dx in (-1, 0, 1):
        for dy in (-1, 0, 1):
            for bt in (0, 1):
                for at in (0, 1):
                    for bs in (0, 1):
                        for as_ in (0, 1):
                            step_x = 2 * dx + bs - bt
                            step_y = 2 * dy + as_ - at
                            if max(abs(step_x), abs(step_y)) >= 2:
                                table[dx + 1, family(bt, at), dy + 1, family(bs, as_)] = far_table(
                                    step_x, step_y
                                )
    return table.reshape(3 * FAMILY, 3 * FAMILY)


def coarse_tables():
    far5 = {}
    to_top = np.zeros((4, LANES, LANES))
    near5 = np.zeros((4, 12, LANES, LANES))
    from_top = np.zeros((4, LANES, LANES))
    lane = lambda column: np.arange(CHAN) * 4 + column
    for row in range(4):
        for column in range(4):
            lift = upward_table(column // 2, row // 2) @ upward_table(column % 2, row % 2)
            to_top[row][np.ix_(lane(column), np.arange(CHAN))] = lift.T
            drop = downward_table(column % 2, row % 2) @ downward_table(column // 2, row // 2)
            from_top[row][np.ix_(np.arange(CHAN), lane(column))] = drop.T
    for row in range(4):
        for column in range(4):
            down = downward_table(column % 2, row % 2)
            x = 4 + column
            for step in range(3):
                for other_row in range(4):
                    for other in range(4):
                        u = 4 * step + other
                        total = np.zeros((CHAN, CHAN))
                        if abs(u // 2 - x // 2) <= 1:
                            if max(abs(u - x), abs(other_row - row)) >= 2:
                                total += far_table(u - x, other_row - row)
                        if abs(u // 2 - x // 2) >= 2:
                            key = (u // 2 - x // 2, other_row // 2 - row // 2)
                            if key not in far5:
                                far5[key] = far_table(*key)
                            total += down @ far5[key] @ upward_table(other % 2, other_row % 2)
                        near5[row, step * 4 + other_row][np.ix_(lane(other), lane(column))] += total.T
    top = np.zeros((LANES, 32 * 32))
    for step in range(-15, 16):
        if abs(step) >= 2:
            top[:CHAN, (step + 15) * 32 : (step + 15) * 32 + CHAN] = far_table(step, 0).T
    return to_top, near5, from_top, top


def halves_np(table):
    high = np.asarray(table, np.float32).astype(jnp.bfloat16)
    low = (np.asarray(table, np.float32) - high.astype(np.float32)).astype(jnp.bfloat16)
    return high, low


def split_lanes():
    table = np.zeros((LANES, LANES), np.float32)
    x = np.arange(LANES)
    table[x, 64 * (x % 2) + x // 2] = 1.0
    return np.concatenate([table, table], axis=0).astype(jnp.bfloat16)


def join_lanes():
    table = np.zeros((2, LANES, LANES), np.float32)
    x = np.arange(64)
    table[0, x, 2 * x] = 1.0
    table[1, x, 2 * x + 1] = 1.0
    table = table.reshape(2 * LANES, LANES)
    return np.concatenate([table, table], axis=0).astype(jnp.bfloat16)


def quarter_lanes():
    k = np.arange(LANES)
    return (k[:, None] % 4 == k[None, :]).astype(np.float32)


def halves(value):
    high = value.astype(bf16)
    return high, (value - high.astype(f32)).astype(bf16)


def dot(left, right):
    return jnp.dot(left, right, preferred_element_type=f32)


def lane_index(rows):
    return lax.broadcasted_iota(jnp.int32, (rows, LANES), 1)


def whole(shape):
    return pl.BlockSpec(shape, lambda *_: (0,) * len(shape))


def upward_kernel(
    after, own, other, split_ref, lift_ref, spread_ref, cells, to_left, to_right, top, bottom, coarse, mom, raw
):
    for tile in range(4):
        rows = pl.ds(8 * tile, 8)

        def add_slot(j, sums):
            for ref in (own, other):
                x, y, re = ref[0, j, rows, :], ref[1, j, rows, :], ref[2, j, rows, :]
                real, imag = list(sums[:ORDER]), list(sums[ORDER:])
                real[0] = real[0] + re
                im = re * y
                re = re * x
                real[1] = real[1] + re
                imag[1] = imag[1] + im
                for k in range(2, ORDER):
                    re, im = re * x - im * y, re * y + im * x
                    real[k] = real[k] + re
                    imag[k] = imag[k] + im
                sums = tuple(real + imag)
            return sums

        sums = lax.fori_loop(
            0, 16, add_slot, tuple(jnp.zeros((8, LANES), f32) for _ in range(CHAN)), unroll=4
        )
        for c in range(CHAN):
            mom[pl.ds(8 * tile * CHAN + c, 8, stride=CHAN), :] = sums[c]

    lane40 = lane_index(40)
    lane80 = lane_index(FAMILY)
    first = jnp.zeros((FAMILY, LANES), f32)
    last = jnp.zeros((FAMILY, LANES), f32)
    ends = [jnp.zeros((FAMILY, LANES), f32)] * 2
    for k, height in enumerate(HEIGHTS):
        source = mom[...] if k == 0 else raw[pl.ds(0, 40 * height), :]
        spread = dot(jnp.concatenate(halves(source), axis=1), split_ref[...])
        parents = []
        for row in range(height):
            block = spread[40 * row : 40 * row + 40]
            even = jnp.where(lane40 < 64, block, 0.0)
            odd = jnp.where(lane40 < 64, pltpu.roll(block, 64, 1), 0.0)
            parent = jnp.concatenate([even, odd], axis=0)
            index = OFFSETS[k] + row
            cells[pl.ds(FAMILY * index, FAMILY), :] = parent
            first = jnp.where(lane80 == index, pltpu.roll(parent, index, 1), first)
            last = jnp.where(
                lane80 == index, pltpu.roll(parent, (index - WIDTHS[k] + 1) % LANES, 1), last
            )
            parents.append(parent)
            for side, ref in enumerate((top, bottom)):
                if row != (height - 1) * side:
                    continue
                if k == 0:
                    ref[pl.ds(104, FAMILY), :] = parent
                else:
                    inside = (lane80 > PACKS[k]) & (lane80 <= PACKS[k] + WIDTHS[k])
                    ends[side] = jnp.where(inside, pltpu.roll(parent, PACKS[k] + 1, 1), ends[side])
        high, low = halves(jnp.concatenate(parents, axis=1))
        lifted = dot(lift_ref[...], jnp.concatenate([high, low, high], axis=0))
        for row in range(height):
            raw[pl.ds(CHAN * row, CHAN), :] = lifted[:CHAN, LANES * row : LANES * (row + 1)]
    to_left[pl.ds(32, FAMILY), :] = first
    to_right[pl.ds(32, FAMILY), :] = last
    for side, ref in enumerate((top, bottom)):
        ref[pl.ds(104 + FAMILY, FAMILY), :] = ends[side]
        ref[pl.ds(96, 8), :] = jnp.zeros((8, LANES), f32)
        for half, source in enumerate((own, other)):
            for comp in range(3):
                for j in range(16):
                    ref[pl.ds(comp * 32 + half * 16 + j, 1), :] = source[comp, j, pl.ds(31 * side, 1), :]

    four = jnp.dot(raw[pl.ds(0, 24), :], spread_ref[...], precision=precise)
    row24 = lax.broadcasted_iota(jnp.int32, (24, LANES), 0)
    line = jnp.sum(jnp.where((lane_index(24) // 4 == row24) & (row24 < CHAN), four, 0.0), axis=0, keepdims=True)
    coarse[...] = jnp.broadcast_to(line, coarse.shape)

    lane32 = lane_index(32)

    left = right = jnp.zeros((32, LANES), f32)
    for half, ref in enumerate((own, other)):
        for comp in range(3):
            for j in range(16):
                m = comp * 32 + half * 16 + j
                value = ref[comp, j]
                left = jnp.where(lane32 == m, pltpu.roll(value, m, 1), left)
                right = jnp.where(lane32 == m, pltpu.roll(value, m + 1, 1), right)
    to_left[pl.ds(0, 32), :] = left
    to_right[pl.ds(0, 32), :] = right


def ring_columns(parent, k, index, from_left, from_right, lane):
    width = WIDTHS[k]
    parent = jnp.where(lane == LANES - 1, pltpu.roll(from_left, (LANES - 1 - index) % LANES, 1), parent)
    return jnp.where(lane == width, pltpu.roll(from_right, (width - index) % LANES, 1), parent)


def rows_kernel(place, after, top, bottom, came_left, came_right, out_top, out_bottom, from_left, from_right):
    lane80 = lane_index(FAMILY)
    from_left[...] = jnp.where(place[0] > 0, came_left[...], 0.0)
    from_right[...] = jnp.where(place[0] < 15, came_right[...], 0.0)
    left, right = from_left[pl.ds(32, FAMILY), :], from_right[pl.ds(32, FAMILY), :]
    for side, (ref, out) in enumerate(((top, out_top), (bottom, out_bottom))):
        out[pl.ds(0, 104), :] = ref[pl.ds(0, 104), :]
        out[pl.ds(96, 1), :] = from_left[pl.ds(31 * side, 1), :]
        out[pl.ds(97, 1), :] = from_right[pl.ds(31 * side, 1), :]
        out[pl.ds(104, FAMILY), :] = ring_columns(
            ref[pl.ds(104, FAMILY), :], 0, 15 * side, left, right, lane80
        )
        packed = ref[pl.ds(104 + FAMILY, FAMILY), :]
        for k in range(1, 5):
            index = OFFSETS[k] + (HEIGHTS[k] - 1) * side
            start = PACKS[k]
            stop = start + WIDTHS[k] + 1
            packed = jnp.where(lane80 == start, pltpu.roll(left, (start - index) % LANES, 1), packed)
            packed = jnp.where(lane80 == stop, pltpu.roll(right, (stop - index) % LANES, 1), packed)
        out[pl.ds(104 + FAMILY, FAMILY), :] = packed


GROUP = 8


def inside_domain(tile, dy):
    return dy == 0 or (dy == -1 and tile > 0) or (dy == 1 and tile < 3)


def add_sources(acc, own, tile, group, sources, count, unroll):
    rows = pl.ds(8 * tile, 8)
    tx = [own[0, group * GROUP + i, rows, :] for i in range(GROUP)]
    ty = [own[1, group * GROUP + i, rows, :] for i in range(GROUP)]

    def pairs(j, acc):
        acc = list(acc)
        for source in sources:
            sx, sy, q = source(j)
            for i in range(GROUP):
                gap_x = tx[i] - sx
                gap_y = ty[i] - sy
                weight = q * (1.0 / (gap_x * gap_x + (gap_y * gap_y + BLOB)))
                acc[i] = acc[i] + weight * gap_x
                acc[GROUP + i] = acc[GROUP + i] + weight * gap_y
        return tuple(acc)

    return lax.fori_loop(0, count, pairs, acc, unroll=unroll)


def store_group(out, acc, tile, group):
    for i in range(GROUP):
        out[0, group * GROUP + i, pl.ds(8 * tile, 8), :] = acc[i]
        out[1, group * GROUP + i, pl.ds(8 * tile, 8), :] = acc[GROUP + i]


def inner_kernel(own, sources, earlier, after, out, *, add):
    for tile in range(4):
        for group in range(16 // GROUP):
            if add:
                acc = tuple(
                    earlier[part, group * GROUP + i, pl.ds(8 * tile, 8), :]
                    for part in range(2)
                    for i in range(GROUP)
                )
            else:
                acc = tuple(jnp.zeros((8, LANES), f32) for _ in range(2 * GROUP))
            steps = []
            for dy in (-1, 0, 1):
                if not inside_domain(tile, dy):
                    continue

                def source(j, rows=pl.ds(8 * tile + dy, 8), dy=dy):
                    y = sources[1, j, rows, :]
                    return sources[0, j, rows, :], y + float(dy) if dy else y, sources[2, j, rows, :]

                steps.append(source)
            acc = add_sources(acc, own, tile, group, steps, 16, 8)
            store_group(out, acc, tile, group)


def near_kernel(
    place, own, other, inner, from_left, from_right, came_above, came_below, out, src, above, below
):
    above[...] = jnp.where(place[1] > 0, came_above[pl.ds(0, 104), :], 0.0)
    below[...] = jnp.where(place[1] < 3, came_below[pl.ds(0, 104), :], 0.0)
    lane32 = lane_index(32)
    lane1 = lane_index(1)

    for comp in range(3):
        for half, ref in enumerate((own, other)):
            for j in range(16):
                m = comp * 32 + half * 16 + j
                rows = (ref[comp, j], above[pl.ds(m, 1), :], below[pl.ds(m, 1), :])
                lefts = (from_left[pl.ds(0, 32), :], above[pl.ds(96, 1), :], below[pl.ds(96, 1), :])
                rights = (from_right[pl.ds(0, 32), :], above[pl.ds(97, 1), :], below[pl.ds(97, 1), :])
                for part in range(3):
                    place = (pl.ds(8, 32), pl.ds(7, 1), pl.ds(40, 1))[part]
                    lane = lane32 if part == 0 else lane1
                    middle = rows[part]
                    before = pltpu.roll(middle, 1, 1)
                    after = pltpu.roll(middle, LANES - 1, 1)
                    left = pltpu.roll(lefts[part], (LANES - m) % LANES, 1)
                    right = pltpu.roll(rights[part], (LANES - 1 - m) % LANES, 1)
                    before = jnp.where(lane == 0, left, before)
                    after = jnp.where(lane == LANES - 1, right, after)
                    if comp == 0:
                        before = before - 1.0
                        after = after + 1.0
                    src[0, m, place, :] = before
                    if part == 0:
                        src[1, m, pl.ds(8, 8), :] = middle[0:8]
                        src[1, m, pl.ds(32, 8), :] = middle[24:32]
                    else:
                        src[1, m, place, :] = middle
                    src[2, m, place, :] = after

    for tile in range(4):
        for group in range(16 // GROUP):
            acc = tuple(
                inner[part, group * GROUP + i, pl.ds(8 * tile, 8), :]
                for part in range(2)
                for i in range(GROUP)
            )
            steps = []
            for dy in (-1, 0, 1):
                for dx in range(3):
                    if dx == 1 and inside_domain(tile, dy):
                        continue

                    def source(j, dx=dx, rows=pl.ds(8 + 8 * tile + dy, 8), dy=dy):
                        y = src[dx, 32 + j, rows, :]
                        return src[dx, j, rows, :], y + float(dy) if dy else y, src[dx, 64 + j, rows, :]

                    steps.append(source)
            acc = add_sources(acc, own, tile, group, steps, 32, 4)
            store_group(out, acc, tile, group)


def three_products(value, table):
    product = dot(jnp.concatenate(halves(value), axis=0), table)
    return product[:16, :LANES] + product[16:, :LANES] + product[:16, LANES:]


def packed_parts(value):
    high = value.astype(bf16).astype(f32)
    low = value - high
    return (high + pltpu.roll(low, 32, 1) + pltpu.roll(high, 64, 1)).astype(bf16)


def side_by_side(table):
    return np.concatenate(halves_np(table), axis=-1)


def packed_table(table):
    high, low = halves_np(table)
    out = np.zeros(table.shape, jnp.bfloat16)
    out[..., 0:32, :] = high[..., 0:32, :]
    out[..., 32:64, :] = high[..., 0:32, :]
    out[..., 64:96, :] = low[..., 0:32, :]
    return out


def far_kernel(
    place, own, near, cells, from_left, from_right, above, below, gathered,
    far_ref, drop_ref, join_ref, spread_ref, to_top, near5, from_top, top_ref,
    out, high, low, fars, paired, joined_ref, loc,
):
    cell = place[0]
    level = place[1]
    tops = three_products(
        jnp.concatenate([gathered[pl.ds(row, 16, stride=4), :] for row in range(4)], axis=1), to_top[...]
    )
    spread = dot(packed_parts(tops), top_ref[...])
    source = lax.broadcasted_iota(jnp.int32, (16, 1024), 0)
    step = lax.broadcasted_iota(jnp.int32, (16, 1024), 1) // 32
    line = jnp.sum(jnp.where(step == source - cell + 15, spread, 0.0), axis=0, keepdims=True)
    total = line[:, :LANES]
    for block in range(1, 8):
        total = total + line[:, LANES * block : LANES * (block + 1)]
    total = jnp.broadcast_to(total, (16, LANES))
    total = total + pltpu.roll(total, 64, 1)
    total = total + pltpu.roll(total, 32, 1)
    total = jnp.where(lane_index(16) < CHAN, total, 0.0)
    around = []
    for step in range(3):
        there = cell + step - 1
        inside = (there >= 0) & (there < 16)
        there = jnp.clip(there, 0, 15)
        for row in range(4):
            value = gathered[pl.ds(there * 4 + row, 1), :]
            around.append(jnp.broadcast_to(jnp.where(inside, value, 0.0), (16, LANES)))
    five = dot(packed_parts(total), from_top[0]) + three_products(
        jnp.concatenate(around, axis=1), near5[0]
    )
    five = jnp.broadcast_to(five[0:1], (32, LANES))
    row32 = lax.broadcasted_iota(jnp.int32, (32, LANES), 0)
    five = jnp.where((lane_index(32) // 4 == row32) & (row32 < CHAN), five, 0.0)
    loc[...] = jnp.zeros(loc.shape, f32)
    loc[pl.ds(0, 32), pl.ds(0, LANES)] = dot(
        jnp.concatenate(halves(five), axis=1), spread_ref[...]
    )

    lane80 = lane_index(FAMILY)
    left, right = from_left[pl.ds(32, FAMILY), :], from_right[pl.ds(32, FAMILY), :]
    start = 0
    starts = []
    for k, height in enumerate(HEIGHTS):
        starts.append(start)
        for row in range(-1, height + 1):
            if row in (-1, height):
                ref = above if row == -1 else below
                inside = level > 0 if row == -1 else level < 3
                if k == 0:
                    parent = ref[pl.ds(104, FAMILY), :]
                else:
                    packed = ref[pl.ds(104 + FAMILY, FAMILY), :]
                    parent = pltpu.roll(packed, LANES - PACKS[k] - 1, 1)
                    parent = jnp.where((lane80 <= WIDTHS[k]) | (lane80 == LANES - 1), parent, 0.0)
            else:
                index = OFFSETS[k] + row
                parent = cells[pl.ds(FAMILY * index, FAMILY), :]
                parent = ring_columns(parent, k, index, left, right, lane80)
            if row in (-1, height):
                parent = jnp.where(inside, parent, 0.0)
            part_high, part_low = halves(parent)
            high[pl.ds(FAMILY * start, FAMILY), :] = part_high
            low[pl.ds(FAMILY * start, FAMILY), :] = part_low
            start += 1

    def far_rows(k, rows):
        both = []
        for ref in (high, low):
            both.append(
                jnp.concatenate(
                    [ref[pl.ds(FAMILY * (starts[k] + row), 3 * FAMILY), :] for row in rows], axis=1
                )
            )
        size = 3 * FAMILY
        product = dot(far_ref[...], both[0])
        product = product[:size] + product[size:] + dot(far_ref[pl.ds(0, size), :], both[1])
        for place_, row in enumerate(rows):
            part = product[:, LANES * place_ : LANES * (place_ + 1)]
            fars[pl.ds(FAMILY * (OFFSETS[k] + row), FAMILY), :] = (
                part[FAMILY : 2 * FAMILY]
                + pltpu.roll(part[:FAMILY], 1, 1)
                + pltpu.roll(part[2 * FAMILY :], LANES - 1, 1)
            )

    for k, height in enumerate(HEIGHTS):
        for row in range(0, height, 2):
            far_rows(k, (row, row + 1) if height > 1 else (row,))

    for k in range(4, -1, -1):
        height = HEIGHTS[k]
        part_high, part_low = halves(loc[:, pl.ds(0, LANES * height)])
        dropped = dot(drop_ref[...], jnp.concatenate([part_high, part_low, part_high], axis=0))
        for row in range(height):
            here = dropped[:, LANES * row : LANES * (row + 1)] + fars[pl.ds(FAMILY * (OFFSETS[k] + row), FAMILY), :]
            paired[pl.ds(40 * row, 40), :] = jnp.concatenate([here[:40], here[40:]], axis=1)
        part_high, part_low = halves(paired[pl.ds(0, 40 * height), :])
        joined = dot(jnp.concatenate([part_high, part_low], axis=1), join_ref[...])
        joined_ref[pl.ds(0, 40 * height), :] = joined
        if k > 0:
            for row in range(2 * height):
                loc[pl.ds(0, CHAN), pl.ds(LANES * row, LANES)] = joined_ref[pl.ds(CHAN * row, CHAN), :]

    scale = 1.0 / (2.0 * math.pi)
    for tile in range(4):
        rows = pl.ds(8 * tile, 8)
        terms = [joined_ref[pl.ds(8 * tile * CHAN + c, 8, stride=CHAN), :] for c in range(CHAN)]

        def value(j, _, terms=terms, rows=rows):
            x, y = own[0, j, rows, :], own[1, j, rows, :]
            re, im = terms[ORDER - 1], terms[CHAN - 1]
            for l in range(ORDER - 2, -1, -1):
                re, im = re * x - im * y + terms[l], re * y + im * x + terms[ORDER + l]
            out[0, j, rows, :] = (im - near[1, j, rows, :]) * scale
            out[1, j, rows, :] = (re + near[0, j, rows, :]) * scale
            return 0

        lax.fori_loop(0, 16, value, 0, unroll=4)


def params():
    return pltpu.CompilerParams(vmem_limit_bytes=VMEM)


def shape(*sizes):
    return jax.ShapeDtypeStruct(sizes, f32)


def neighbours(value, axis, step):
    size = lax.axis_size(axis)
    return lax.ppermute(value, axis, [(i, (i + step) % size) for i in range(size)])


def fields(own, place):
    smem = pl.BlockSpec(memory_space=pltpu.SMEM)
    vmem = pl.BlockSpec(memory_space=pltpu.VMEM)
    anywhere = pl.BlockSpec(memory_space=pl.ANY)
    other = lax.ppermute(own, "rep", [(0, 1), (1, 0)])
    inner = pl.pallas_call(
        lambda own, out: inner_kernel(own, own, None, None, out, add=False),
        out_shape=shape(2, 16, 32, LANES),
        compiler_params=params(),
        name="inner_own",
    )(own)
    lift_high, lift_low = halves_np(upward_family())
    lift = np.zeros((32, 3 * FAMILY), jnp.bfloat16)
    lift[:CHAN] = np.concatenate([lift_high, lift_high, lift_low], axis=1)
    message = shape(104 + 2 * FAMILY, LANES)
    sides = shape(32 + FAMILY, LANES)
    cells, to_left, to_right, top, bottom, coarse = pl.pallas_call(
        upward_kernel,
        in_specs=[anywhere] + [vmem] * 5,
        out_shape=(shape(ROWS * FAMILY, LANES), sides, sides, message, message, shape(64, LANES)),
        scratch_shapes=[pltpu.VMEM((640, LANES), f32), pltpu.VMEM((320, LANES), f32)],
        compiler_params=params(),
        name="upward",
    )(inner, own, other, jnp.asarray(split_lanes()), jnp.asarray(lift), jnp.asarray(quarter_lanes().T.copy()))
    from_left = neighbours(to_right, "cell", 1)
    from_right = neighbours(to_left, "cell", -1)
    gathered = lax.all_to_all(coarse, ("cell", "level"), 0, 0, tiled=True)
    inner = pl.pallas_call(
        functools.partial(inner_kernel, add=True),
        in_specs=[vmem] * 3 + [anywhere],
        out_shape=shape(2, 16, 32, LANES),
        compiler_params=params(),
        name="inner",
    )(own, other, inner, cells)
    top, bottom, from_left, from_right = pl.pallas_call(
        rows_kernel,
        in_specs=[smem, anywhere] + [vmem] * 4,
        out_shape=(message, message, sides, sides),
        compiler_params=params(),
        name="rows",
    )(place, inner, top, bottom, from_left, from_right)
    above = neighbours(bottom, "level", 1)
    below = neighbours(top, "level", -1)
    near = pl.pallas_call(
        near_kernel,
        in_specs=[smem] + [vmem] * 7,
        out_shape=shape(2, 16, 32, LANES),
        scratch_shapes=[
            pltpu.VMEM((3, 96, 48, LANES), f32),
            pltpu.VMEM((104, LANES), f32),
            pltpu.VMEM((104, LANES), f32),
        ],
        compiler_params=params(),
        name="near",
    )(place, own, other, inner, from_left, from_right, above, below)
    far_high, far_low = halves_np(far_family())
    drop_table = np.zeros((FAMILY, 32))
    drop_table[:, :CHAN] = downward_family()
    drop_high, drop_low = halves_np(drop_table)
    to_top, near5, from_top, top = coarse_tables()
    tables = [
        np.concatenate([far_high, far_low], axis=0),
        np.concatenate([drop_high, drop_high, drop_low], axis=1),
        join_lanes(),
        np.concatenate([quarter_lanes()] * 2, axis=0).astype(jnp.bfloat16),
        side_by_side(to_top.reshape(4 * LANES, LANES)),
        side_by_side(near5.reshape(4, 12 * LANES, LANES)),
        packed_table(from_top),
        packed_table(top),
    ]
    operands = [own, near, cells, from_left, from_right, above, below, gathered] + [
        jnp.asarray(table) for table in tables
    ]
    specs = [whole(value.shape) for value in operands]
    specs[13] = pl.BlockSpec((1, 12 * LANES, 2 * LANES), lambda i, place: (place[1], 0, 0))
    specs[14] = pl.BlockSpec((1, LANES, LANES), lambda i, place: (place[1], 0, 0))
    return pl.pallas_call(
        far_kernel,
        grid_spec=pltpu.PrefetchScalarGridSpec(
            num_scalar_prefetch=1,
            grid=(1,),
            in_specs=specs,
            out_specs=whole((2, 16, 32, LANES)),
            scratch_shapes=[
                pltpu.VMEM((41 * FAMILY, LANES), bf16),
                pltpu.VMEM((41 * FAMILY, LANES), bf16),
                pltpu.VMEM((ROWS * FAMILY, LANES), f32),
                pltpu.VMEM((640, 2 * LANES), f32),
                pltpu.VMEM((640, LANES), f32),
                pltpu.VMEM((32, 16 * LANES), f32),
            ],
        ),
        out_shape=shape(2, 16, 32, LANES),
        compiler_params=params(),
        name="far",
    )(place, *operands)


def flat_index(shape_):
    rows = lax.broadcasted_iota(jnp.int32, shape_, 0)
    return rows * LANES + lax.broadcasted_iota(jnp.int32, shape_, 1)


def swap_step(arrays, bit, high, descending, lanes):
    distance = 1 << bit

    def partner(value):
        if distance >= LANES:
            step = distance // LANES
            down = pltpu.roll(value, step, 0)
            return down if step == 4 else jnp.where(high, down, pltpu.roll(value, 8 - step, 0))
        if distance == 64:
            return pltpu.roll(value, 64, 1)
        return jnp.take_along_axis(value, lanes ^ distance, axis=1)

    key = arrays[0]
    other = partner(key)
    flip = high if descending is False else (~high if descending is True else high ^ descending)
    take = (other < key) ^ flip
    return [jnp.where(take, other, key)] + [jnp.where(take, partner(x), x) for x in arrays[1:]]


def bitonic(tiles, first_block, last_block):
    index = flat_index((8, LANES))
    lanes = lax.broadcasted_iota(jnp.int32, (8, LANES), 1)
    highs = [(index & (1 << bit)) != 0 for bit in range(10)]
    count = len(tiles)
    for block in range(first_block, last_block + 1):

        def descending(v):
            if block == last_block:
                return False
            return bool((v >> (block - 10)) & 1) if block >= 10 else highs[block]

        for bit in range(block - 1, -1, -1):
            if bit >= 10:
                step = 1 << (bit - 10)
                for v in range(count):
                    if v & step:
                        continue
                    low, high = tiles[v], tiles[v + step]
                    take = high[0] > low[0] if descending(v) else high[0] < low[0]
                    tiles[v] = [jnp.where(take, y, x) for x, y in zip(low, high)]
                    tiles[v + step] = [jnp.where(take, x, y) for x, y in zip(low, high)]
            else:
                for v in range(count):
                    tiles[v] = swap_step(tiles[v], bit, highs[bit], descending(v), lanes)
    return tiles


def pack_kernel(pos, strength, owner_ref, leaf, slot, out, keys, values):
    owner = owner_ref[...]
    address = slot[...] * 4096 + leaf[...]
    key = owner * 65536 + address
    starts = []
    for o in range(16):
        before = (owner < o).astype(jnp.int32)
        before = before[0:8] + before[8:16] + before[16:24] + before[24:32]
        starts.append(jnp.sum(before))
    loads = (key, pos[0], pos[1], strength[...])
    tiles = bitonic([[load[8 * v : 8 * v + 8] for load in loads] for v in range(4)], 1, 12)
    keys[...] = jnp.full(keys.shape, -1, jnp.int32)
    for v in range(4):
        keys[pl.ds(8 * v, 8), :] = tiles[v][0]
        for c in range(3):
            values[c, pl.ds(8 * v, 8), :] = tiles[v][1 + c]
    lane = lane_index(8)
    for o in range(16):
        start = starts[o]
        row = start // LANES
        shift = start % LANES
        back = jnp.where(shift == 0, 0, LANES - shift)

        def window(ref):
            mixed = jnp.where(lane < shift, ref[pl.ds(row + 1, 8), :], ref[pl.ds(row, 8), :])
            return pltpu.roll(mixed, back, 1)

        mine = window(keys)
        place = mine - o * 65536
        valid = (place >= 0) & (place < 65536)
        out[o, 3] = jnp.where(valid, place, 65536).astype(f32)
        for c in range(3):
            out[o, c] = window(values.at[c])


def settle_kernel(arrived, pos, strength, out, marks_a, marks_b, loads_a, loads_b):
    tiles = [[arrived[v, c] for c in (3, 0, 1, 2)] for v in range(16)]
    turned = [lax.broadcasted_iota(jnp.int32, (8, LANES), axis) for axis in (0, 1)]
    for v in range(1, 16, 2):
        for c in range(4):
            value = jnp.take_along_axis(tiles[v][c], 7 - turned[0], axis=0)
            tiles[v][c] = jnp.take_along_axis(value, LANES - 1 - turned[1], axis=1)
    tiles = bitonic(tiles, 11, 14)
    index = flat_index((8, LANES))
    for ref in (marks_a, marks_b):
        ref[...] = jnp.zeros(ref.shape, jnp.int32)
    for v in range(16):
        address = tiles[v][0].astype(jnp.int32)
        rows = pl.ds(64 + 8 * v, 8)
        marks_a[rows, :] = jnp.where(address < 65536, 2 * (address - index - 1024 * v) + 1, 0)
        for c in range(3):
            loads_a[c, rows, :] = tiles[v][1 + c]
    lane = lane_index(64)
    marks, values = (marks_a, marks_b), (loads_a, loads_b)
    for bit in range(15, -1, -1):
        now, later = marks[bit % 2 == 0], marks[bit % 2]
        load_now, load_later = values[bit % 2 == 0], values[bit % 2]
        test = 2 << bit
        rows = (1 << bit) // LANES
        for base in range(0, 512, 64):
            here = pl.ds(base + 64, 64)
            own = now[here, :]
            own = jnp.where((own & test) != 0, 0, own)
            if rows >= 64 and base < rows:
                later[here, :] = own
                for c in range(3):
                    load_later[c, here, :] = load_now[c, here, :]
                continue

            def source(ref):
                if rows:
                    return ref[pl.ds(base + 64 - rows, 64), :]
                mixed = jnp.where(
                    lane >= LANES - (1 << bit), ref[pl.ds(base + 63, 64), :], ref[here, :]
                )
                return pltpu.roll(mixed, 1 << bit, 1)

            there = source(now)
            come = (there & test) != 0
            later[here, :] = jnp.where(come, there, own)
            for c in range(3):
                load_later[c, here, :] = jnp.where(come, source(load_now.at[c]), load_now[c, here, :])
    for j in range(16):
        rows = pl.ds(64 + 32 * j, 32)
        moved = marks_a[rows, :] != 0
        out[0, j] = jnp.where(moved, loads_a[0, rows, :], pos[0, j])
        out[1, j] = jnp.where(moved, loads_a[1, rows, :], pos[1, j])
        out[2, j] = jnp.where(moved, loads_a[2, rows, :], strength[j])


def local(
    resident_pos, resident_strength, mover_pos, mover_strength, mover_owner, mover_leaf, mover_slot
):
    place = jnp.stack([lax.axis_index("cell"), lax.axis_index("level")]).astype(jnp.int32)
    outgoing = pl.pallas_call(
        pack_kernel,
        out_shape=shape(16, 4, 8, LANES),
        scratch_shapes=[pltpu.VMEM((56, LANES), jnp.int32), pltpu.VMEM((3, 56, LANES), f32)],
        compiler_params=params(),
        name="pack",
    )(
        mover_pos.reshape(2, 32, LANES),
        mover_strength.reshape(32, LANES),
        mover_owner.reshape(32, LANES),
        mover_leaf.reshape(32, LANES),
        mover_slot.reshape(32, LANES),
    )
    arrived = lax.all_to_all(outgoing, "cell", 0, 0, tiled=True)
    own = pl.pallas_call(
        settle_kernel,
        out_shape=shape(3, 16, 32, LANES),
        scratch_shapes=[
            pltpu.VMEM((576, LANES), jnp.int32),
            pltpu.VMEM((576, LANES), jnp.int32),
            pltpu.VMEM((3, 576, LANES), f32),
            pltpu.VMEM((3, 576, LANES), f32),
        ],
        compiler_params=params(),
        name="settle",
    )(arrived, resident_pos, resident_strength)
    return fields(own, place)


def solution(mesh):
    return jax.shard_map(
        local,
        mesh=mesh,
        in_specs=(
            P(None, "rep", "level", "cell"),
            P("rep", "level", "cell"),
            P(None, "rep", "level", "cell"),
            P("rep", "level", "cell"),
            P("rep", "level", "cell"),
            P("rep", "level", "cell"),
            P("rep", "level", "cell"),
        ),
        out_specs=P(None, "rep", "level", "cell"),
        check_vma=False,
    )
```
